32 devices in a mesh: tile: 32 (over z, y, x, core).
Axes of the slice: x: 2, y: 2, z: 4, core: 2. Of those that a mesh axis runs over, the one named last changes fastest.
Arguments:
- fields: float32 [64, 144, 800], P('tile'), may hold values from -6 to 6
- cotangent: float32 [64, 144, 800], P('tile'), may hold values from -6 to 6
- kernel: float32 [49, 800], replicated, may hold values from -0.875 to 0.875
- norm_gain: float32 [800], replicated, may hold values from 0.5 to 1.5
- norm_shift: float32 [800], replicated, may hold values from -3 to 3
- weight_in: bfloat16 [800, 3200], replicated, may hold values from -0.21875 to 0.21875
- bias_in: float32 [3200], replicated, may hold values from -3 to 3
- weight_out: bfloat16 [3200, 800], replicated, may hold values from -0.109375 to 0.109375
- bias_out: float32 [800], replicated, may hold values from -3 to 3
- neighbours: int32 [64, 8], P('tile'), may hold values from -1 to 63, as said below
- land_mask: int32 [64, 144], P('tile'), may hold values from 0 to 1, as said below
Outputs:
- block_out: float32 [64, 144, 800], P('tile')
- fields_grad: float32 [64, 144, 800], P('tile')
- kernel_grad: float32 [49, 800], replicated
- gain_grad: float32 [800], replicated
- shift_grad: float32 [800], replicated
- weight_in_grad: float32 [256, 10000], P('tile')
- bias_in_grad: float32 [3200], replicated
- weight_out_grad: float32 [256, 10000], P('tile')
- bias_out_grad: float32 [800], replicated
The draws below stay inside these ranges and needn't reach their ends.
Inputs may be any that keep to these rules, and one draw needn't show every extreme that they name: `land_mask`: slots that hold an ocean tile come first on each device, and a slot holds one exactly where its row has a one (its cell 0 is then ocean). Each device holds 1 to 1 tiles, some device exactly 1; device i and device i + 16 together hold exactly 2. `neighbours`: an entry is the global slot (device times 2 plus slot) of the neighbouring ocean tile, or -1 for land, the grid's edge and empty slots. Ocean tiles run in grid order over devices and slots, so a neighbour lies at most 7 devices away, and in every draw some lie exactly that far.
All inputs are finite; a program needn't handle non-finite values.
Results may differ from the reference program's by a relative error of at most 0.0055.
Values may be sent and summed in bfloat16 or wider, within the bound.
A program may use at most 192 MiB of HBM per device.

```python
import jax
import jax.numpy as jnp
from jax import lax

CHANNELS = 800
HIDDEN_SIZE = 3200
TILE_SLOTS = 2
GRID_COLS = 6
TILE_SIDE = 12
KERNEL = 7
CELLS = 144
SLOTS_ALL = 64
GRAD_ROWS = 256
GRAD_COLS = 10000
N_TILE = 32


STEPS_AROUND = ((-1, -1), (-1, 0), (-1, 1), (0, -1), (0, 1), (1, -1), (1, 0), (1, 1))


def ocean_layout(key):
    half = N_TILE // 2
    count_key, run_key, gap_key = jax.random.split(key, 3)
    lower = jax.random.randint(count_key, (half,), 1, TILE_SLOTS)
    first = jax.random.randint(run_key, (), 0, half - GRID_COLS - 3)
    places = jnp.arange(half)
    in_run = (places >= first) & (places < first + GRID_COLS + 3)
    lower = jnp.where(in_run, 1, lower)
    counts = jnp.concatenate([lower, TILE_SLOTS - lower]).astype(jnp.int32)
    starts = (jnp.cumsum(counts) - counts).astype(jnp.int32)
    ocean_tiles = N_TILE * TILE_SLOTS // 2
    tiles = jnp.arange(ocean_tiles)
    gaps = (jax.random.randint(gap_key, (ocean_tiles,), 0, 4) == 0).astype(jnp.int32)
    run_tile = starts[first]
    gaps = jnp.where((tiles >= run_tile) & (tiles < run_tile + GRID_COLS + 2), 0, gaps)
    spots = (tiles + jnp.cumsum(gaps) - gaps).astype(jnp.int32)
    return (counts, starts, spots)


def slot_table(counts, starts):
    slot_ids = jnp.arange(N_TILE * TILE_SLOTS)
    owners = slot_ids // TILE_SLOTS
    within = slot_ids % TILE_SLOTS
    held = within < counts[owners]
    tile_ids = jnp.clip(starts[owners] + within, 0, N_TILE * TILE_SLOTS // 2 - 1)
    return (held, tile_ids)


def draw_neighbours(key, part):
    counts, starts, spots = ocean_layout(key)
    held, tile_ids = slot_table(counts, starts)
    ocean_tiles = spots.shape[0]
    spot = spots[tile_ids]
    row_index = spot // GRID_COLS
    col_index = spot % GRID_COLS
    columns = []
    for row_step, col_step in STEPS_AROUND:
        target_col = col_index + col_step
        target_row = row_index + row_step
        target = target_row * GRID_COLS + target_col
        found = jnp.clip(jnp.searchsorted(spots, target), 0, ocean_tiles - 1).astype(jnp.int32)
        valid = held & (target_col >= 0) & (target_col < GRID_COLS) & (target_row >= 0) & (spots[found] == target)
        owner = (jnp.searchsorted(starts, found, side='right') - 1).astype(jnp.int32)
        slot_id = owner * TILE_SLOTS + found - starts[owner]
        columns.append(jnp.where(valid, slot_id, -1))
    return jnp.stack(columns, axis=1).astype(jnp.int32)


def draw_land_mask(key, part):
    counts, starts, spots = ocean_layout(key)
    held, tile_ids = slot_table(counts, starts)
    key = jax.random.fold_in(key, 7)
    cells = jax.random.randint(key, (N_TILE * TILE_SLOTS, TILE_SIDE * TILE_SIDE), 0, 4) > 0
    first_cell = jnp.arange(TILE_SIDE * TILE_SIDE)[None, :] == 0
    return ((cells | first_cell) & held[:, None]).astype(jnp.int32)


def block_levels(key, shape, cuts, low, top_value):
    factor_of = 1.0
    for dim, parts in cuts:
        draws = jax.random.uniform(jax.random.fold_in(jax.random.fold_in(key, 6), dim), (parts,), jnp.float32, low / len(cuts), top_value / len(cuts))
        factor_of = factor_of * jnp.repeat(jnp.exp(draws), shape[dim] // parts).reshape((-1,) + (1,) * (len(shape) - 1 - dim))
    return factor_of


def normal_values(own_key, shape, scale, bound, cuts=(), kind=jnp.bfloat16):
    result = scale * jax.random.normal(own_key, shape, jnp.float32)
    if cuts:
        result = result * block_levels(own_key, shape, cuts, -0.22, 0.18)
    return jnp.clip(result, -bound, bound).astype(kind)


def setup_inputs(seed: int = 0) -> dict:
    arg_keys = jax.random.split(jax.random.key(seed), 12)
    fields = normal_values(arg_keys[0], (SLOTS_ALL, CELLS, CHANNELS), 1.0, 6.0, ((0, 32),), jnp.float32)
    cotangent = normal_values(arg_keys[1], (SLOTS_ALL, CELLS, CHANNELS), 1.0, 6.0, ((0, 32),), jnp.float32)
    kernel = normal_values(arg_keys[2], (KERNEL * KERNEL, CHANNELS), (KERNEL * KERNEL) ** -0.5, 0.875, (), jnp.float32)
    norm_gain = jnp.clip(1.0 + 0.1 * jax.random.normal(arg_keys[3], (CHANNELS,), jnp.float32), 0.5, 1.5)
    norm_shift = normal_values(arg_keys[4], (CHANNELS,), 0.5, 3.0, (), jnp.float32)
    weight_in = normal_values(arg_keys[5], (CHANNELS, HIDDEN_SIZE), CHANNELS ** -0.5, 0.21875)
    bias_in = normal_values(arg_keys[6], (HIDDEN_SIZE,), 0.5, 3.0, (), jnp.float32)
    weight_out = normal_values(arg_keys[7], (HIDDEN_SIZE, CHANNELS), HIDDEN_SIZE ** -0.5, 0.109375)
    bias_out = normal_values(arg_keys[8], (CHANNELS,), 0.5, 3.0, (), jnp.float32)
    neighbours = draw_neighbours(jax.random.fold_in(arg_keys[11], 71), 0)
    land_mask = draw_land_mask(jax.random.fold_in(arg_keys[11], 71), 0)
    return dict(fields=fields, cotangent=cotangent, kernel=kernel, norm_gain=norm_gain, norm_shift=norm_shift, weight_in=weight_in, bias_in=bias_in, weight_out=weight_out, bias_out=bias_out, neighbours=neighbours, land_mask=land_mask)


EPSILON = 1e-05
SQRT_HALF = 0.7071067811865476

@jax.custom_vjp
def low(v):
    return lax.optimization_barrier(v.astype(jnp.bfloat16)).astype(jnp.float32)

@jax.custom_vjp
def low_back(v):
    return v

def low_keep(v):
    return (low(v), None)

def low_pass(kept, grad):
    return (grad,)

def back_keep(v):
    return (v, None)

def back_low(kept, grad):
    return (low(grad),)
low.defvjp(low_keep, low_pass)
low_back.defvjp(back_keep, back_low)

def gelu_value(pre):
    return 0.5 * pre * (1.0 + lax.erf(pre * SQRT_HALF))

def pad_tiles(centre, nearby):
    margin = KERNEL // 2
    upper_rows = jnp.concatenate([nearby[:, 0, -margin:, -margin:], nearby[:, 1, -margin:, :], nearby[:, 2, -margin:, :margin]], axis=2)
    middle = jnp.concatenate([nearby[:, 3, :, -margin:], centre, nearby[:, 4, :, :margin]], axis=2)
    bottom = jnp.concatenate([nearby[:, 5, :margin, -margin:], nearby[:, 6, :margin, :], nearby[:, 7, :margin, :margin]], axis=2)
    return jnp.concatenate([upper_rows, middle, bottom], axis=1)

def depthwise(centre, nearby, kernel):
    padded = pad_tiles(centre, nearby)
    tile_side = centre.shape[1]
    summed = jnp.zeros(centre.shape, centre.dtype)
    for row_tap in range(KERNEL):
        for col_tap in range(KERNEL):
            summed = summed + kernel[row_tap * KERNEL + col_tap] * padded[:, row_tap:row_tap + tile_side, col_tap:col_tap + tile_side]
    return summed

def group_size():
    return 16 if N_TILE % 16 == 0 else 1

def convolve_all(fields, kernel, links):
    group = group_size()
    width = fields.shape[-1]
    span = group * TILE_SLOTS
    padded_fields = jnp.concatenate([fields, jnp.zeros((1,) + fields.shape[1:], fields.dtype)], axis=0)
    safe_links = jnp.where(links < 0, SLOTS_ALL, links).astype(jnp.int32)

    def one_block(start):
        centre = lax.dynamic_slice_in_dim(fields, start, span, 0).reshape(span, TILE_SIDE, TILE_SIDE, width)
        picks = lax.dynamic_slice_in_dim(safe_links, start, span, 0).reshape(-1)
        nearby = jnp.take(padded_fields, picks, axis=0).reshape(span, 8, TILE_SIDE, TILE_SIDE, width)
        return depthwise(centre, nearby, kernel).reshape(span, CELLS, width)
    starts = jnp.arange(N_TILE // group, dtype=jnp.int32) * span
    return lax.map(jax.checkpoint(one_block), starts).reshape(fields.shape)

def feed_all(normed, weight_in, bias_in, weight_out, bias_out):
    group = group_size()
    blocks = normed.reshape(N_TILE // group, group * TILE_SLOTS * CELLS, normed.shape[-1])

    def one_block(block_rows):
        pre = low_back(jnp.dot(block_rows, weight_in, precision=lax.Precision.HIGHEST) + bias_in)
        act = low(gelu_value(pre))
        return low_back(jnp.dot(act, weight_out, precision=lax.Precision.HIGHEST) + bias_out)
    return lax.map(jax.checkpoint(one_block), blocks).reshape(normed.shape)

def block_forward(fields, kernel, norm_gain, norm_shift, weight_in, bias_in, weight_out, bias_out, links, ocean):
    conv = convolve_all(fields, kernel, links)
    cell_weight = ocean[:, :, None]
    ocean_count = jnp.sum(ocean)
    centre_mean = lax.optimization_barrier(jnp.sum(conv * cell_weight, axis=(0, 1))) / ocean_count
    spread = lax.optimization_barrier(jnp.sum(jnp.square(conv - centre_mean) * cell_weight, axis=(0, 1))) / ocean_count
    scaled = (conv - centre_mean) * lax.rsqrt(spread + EPSILON)
    normed = low(scaled * norm_gain + norm_shift)
    branch = feed_all(normed, weight_in, bias_in, weight_out, bias_out)
    return (fields + branch) * cell_weight

def reference(fields, cotangent, kernel, norm_gain, norm_shift, weight_in, bias_in, weight_out, bias_out, neighbours, land_mask):
    ocean = land_mask.astype(jnp.float32)

    def forward(field_in, kernel_in, gain_in, shift_in, weight_first, bias_first, weight_second, bias_second):
        return block_forward(field_in, kernel_in, gain_in, shift_in, weight_first, bias_first, weight_second, bias_second, neighbours, ocean)
    block_out, pullback = jax.vjp(forward, fields, kernel, norm_gain, norm_shift, weight_in.astype(jnp.float32), bias_in, weight_out.astype(jnp.float32), bias_out)
    grads = pullback(cotangent)
    return (block_out, grads[0], grads[1], grads[2], grads[3], grads[4].reshape(GRAD_ROWS, GRAD_COLS), grads[5], grads[6].reshape(GRAD_ROWS, GRAD_COLS), grads[7])
```

```python
import functools
import math

import jax
import jax.numpy as jnp
from jax import lax
from jax.experimental import pallas as pl
from jax.experimental.pallas import tpu as pltpu
from jax.sharding import PartitionSpec as P

TILE_SIDE = 12
KERNEL = 7
CELLS = 144
REACH = 7
MARGIN = KERNEL // 2
PAD_SIDE = TILE_SIDE + 2 * MARGIN
EDGE = MARGIN * TILE_SIDE
INNER = 8
LANES = 128
SUB = 8

EPSILON = 1e-05
SQRT_HALF = 0.7071067811865476
INV_ROOT_TAU = 0.3989422804014327
BF = jnp.bfloat16
F32 = jnp.float32
MESH = pl.DeviceIdType.MESH
NN = (((1,), (0,)), ((), ()))
NT = (((1,), (1,)), ((), ()))


def dot(a, b, dims=NN, precision=None):
    return lax.dot_general(a, b, dims, preferred_element_type=F32, precision=precision)


def window(start, need, total):
    width = min(total, (-(-(need + LANES - 1) // LANES)) * LANES)
    first = jnp.minimum((start // LANES) * LANES, total - width)
    return first, width


def step_kernel(
    N,
    C,
    H,
    fields_hbm,
    cot_hbm,
    kernel_ref,
    gain_ref,
    shift_ref,
    win_hbm,
    bin_ref,
    wout_hbm,
    bout_ref,
    nbr_ref,
    mask_ref,
    maskv_ref,
    o_block,
    o_fgrad,
    o_kgrad,
    o_vec,
    o_win,
    o_wout,
    x_nat,
    cot_nat,
    win,
    wout,
    xc,
    pad,
    conv,
    ngc,
    kc,
    gc,
    strip_top,
    strip_bot,
    strip_lef,
    strip_rig,
    from_low,
    from_high,
    from_w,
    from_e,
    stat_a,
    stat_b,
    stat_sa,
    stat_sb,
    nrm,
    ups,
    actg,
    branch,
    nall,
    uall,
    wi_t,
    wo_t,
    bi_t,
    act_t,
    pg_t,
    og,
    ig,
    zo_src,
    zi_src,
    zo_dst,
    zi_dst,
    tr,
    tr_src,
    tr_dst,
    kg,
    kg_slot,
    kg_col,
    kg_tot,
    load_sem,
    halo_send,
    halo_recv,
    vec_send,
    vec_recv,
    col_send,
    col_recv,
    rows_send,
    rows_recv,
    z_send,
    z_recv,
    tr_send,
    tr_recv,
    ks_send,
    ks_recv,
):
    Q = N // INNER
    hb = H // N
    cb = C // N
    LT = -(-C // LANES)
    tail = C - (LT - 1) * LANES
    me = lax.axis_index("tile")
    p = lax.rem(me, INNER)
    q = me // INNER

    def remote(src, dst, ssem, rsem, dev):
        return pltpu.make_async_remote_copy(
            src_ref=src, dst_ref=dst, send_sem=ssem, recv_sem=rsem, device_id=(dev,), device_id_type=MESH
        )

    def in_plane(s):
        return q * INNER + lax.rem(p + s, INNER)

    def in_column(t):
        return lax.rem(q + t, Q) * INNER + p

    loads = [
        pltpu.make_async_copy(fields_hbm.at[0], x_nat, load_sem.at[0]),
        pltpu.make_async_copy(cot_hbm.at[0], cot_nat, load_sem.at[1]),
        pltpu.make_async_copy(wout_hbm, wout, load_sem.at[2]),
        pltpu.make_async_copy(win_hbm, win, load_sem.at[3]),
    ]
    for copy in loads:
        copy.start()
    barrier = pltpu.get_barrier_semaphore()

    @pl.loop(1, REACH + 1)
    def _(k):
        @pl.when(me + k < N)
        def _():
            pl.semaphore_signal(barrier, inc=1, device_id=(me + k,), device_id_type=MESH)

        @pl.when(me - k >= 0)
        def _():
            pl.semaphore_signal(barrier, inc=1, device_id=(me - k,), device_id_type=MESH)

    @pl.loop(1, Q)
    def _(t):
        pl.semaphore_signal(barrier, inc=1, device_id=(in_column(t),), device_id_type=MESH)

    def cells_from(dst, tile_of, count):
        for t in range(SUB):
            if t < LT:
                v = tile_of(t)
                if t == LT - 1 and tail < LANES:
                    v = jnp.concatenate([v, jnp.zeros((count, LANES - tail), F32)], axis=1)
            else:
                v = jnp.zeros((count, LANES), F32)
            dst[pl.ds(t, count, stride=SUB), :] = v

    def lanes(t):
        return slice(t * LANES, min((t + 1) * LANES, C))

    cells_from(kc, lambda t: kernel_ref[:, lanes(t)], KERNEL * KERNEL)
    for t in range(SUB):
        for row, ref in ((0, gain_ref), (1, shift_ref)):
            if t < LT:
                v = ref[:, lanes(t)]
                if t == LT - 1 and tail < LANES:
                    v = jnp.concatenate([v, jnp.zeros((1, LANES - tail), F32)], axis=1)
            else:
                v = jnp.zeros((1, LANES), F32)
            gc[row * SUB + t : row * SUB + t + 1, :] = v

    loads[0].wait()
    cells_from(xc, lambda t: x_nat[:, lanes(t)], CELLS)

    def make_strips(src):
        strip_top[...] = src[0 : EDGE * SUB, :].astype(BF)
        strip_bot[...] = src[(CELLS - EDGE) * SUB : CELLS * SUB, :].astype(BF)
        lef, rig = [], []
        for r in range(TILE_SIDE):
            row = r * TILE_SIDE * SUB
            lef.append(src[row : row + MARGIN * SUB, :])
            rig.append(src[row + (TILE_SIDE - MARGIN) * SUB : row + TILE_SIDE * SUB, :])
        strip_lef[...] = jnp.concatenate(lef, axis=0).astype(BF)
        strip_rig[...] = jnp.concatenate(rig, axis=0).astype(BF)

    def halo_up(e, k):
        return remote(strip_bot, from_low.at[e, k], halo_send.at[e, 0, k], halo_recv.at[e, 0, k], me + k)

    def halo_down(e, k):
        return remote(strip_top, from_high.at[e, k], halo_send.at[e, 1, k], halo_recv.at[e, 1, k], me - k)

    def halo_east(e):
        return remote(strip_rig, from_w.at[e, 1], halo_send.at[e, 0, 0], halo_recv.at[e, 0, 0], me + 1)

    def halo_west(e):
        return remote(strip_lef, from_e.at[e, 1], halo_send.at[e, 1, 0], halo_recv.at[e, 1, 0], me - 1)

    def halo_start(e):
        @pl.loop(1, REACH + 1)
        def _(k):
            @pl.when(me + k < N)
            def _():
                halo_up(e, k).start()

            @pl.when(me - k >= 0)
            def _():
                halo_down(e, k).start()

        @pl.when(me + 1 < N)
        def _():
            halo_east(e).start()

        @pl.when(me >= 1)
        def _():
            halo_west(e).start()

    def halo_wait(e):
        @pl.loop(1, REACH + 1)
        def _(k):
            @pl.when(me + k < N)
            def _():
                halo_up(e, k).wait_send()
                halo_down(e, k).wait_recv()

            @pl.when(me - k >= 0)
            def _():
                halo_down(e, k).wait_send()
                halo_up(e, k).wait_recv()

        @pl.when(me + 1 < N)
        def _():
            halo_east(e).wait_send()
            halo_west(e).wait_recv()

        @pl.when(me >= 1)
        def _():
            halo_west(e).wait_send()
            halo_east(e).wait_recv()

    zero_strip = jnp.zeros((EDGE * SUB, LANES), BF)
    for e in range(2):
        from_low[e, 0] = zero_strip
        from_high[e, 0] = zero_strip
        from_w[e, 0] = zero_strip
        from_e[e, 0] = zero_strip

    def fill_pad(e, centre):
        def low_slot(d):
            n = nbr_ref[0, d]
            return jnp.clip(jnp.where(n < 0, 0, me - lax.shift_right_arithmetic(n, 1)), 0, REACH)

        def high_slot(d):
            n = nbr_ref[0, d]
            return jnp.clip(jnp.where(n < 0, 0, lax.shift_right_arithmetic(n, 1) - me), 0, REACH)

        def there(d):
            return jnp.where(nbr_ref[0, d] < 0, 0, 1)

        def put(row, col, value):
            at = (row * PAD_SIDE + col) * SUB
            pad[at : at + value.shape[0], :] = value

        S, M, T = SUB, MARGIN, TILE_SIDE
        for which, refs, slot, d3, row0 in (
            ("low", from_low, low_slot, (0, 1, 2), 0),
            ("high", from_high, high_slot, (5, 6, 7), M + T),
        ):
            left = refs[e, slot(d3[0])].astype(F32)
            mid = refs[e, slot(d3[1])].astype(F32)
            right = refs[e, slot(d3[2])].astype(F32)
            for r in range(M):
                at = r * T * S
                put(row0 + r, 0, left[at + (T - M) * S : at + T * S])
                put(row0 + r, M, mid[at : at + T * S])
                put(row0 + r, M + T, right[at : at + M * S])
        west = from_w[e, there(3)].astype(F32)
        east = from_e[e, there(4)].astype(F32)
        for r in range(T):
            put(M + r, 0, west[r * M * S : (r + 1) * M * S])
            put(M + r, M, centre[r * T * S : (r + 1) * T * S, :])
            put(M + r, M + T, east[r * M * S : (r + 1) * M * S])

    make_strips(xc)
    n_partners = jnp.minimum(REACH, N - 1 - me) + jnp.minimum(REACH, me) + (Q - 1)
    pl.semaphore_wait(barrier, n_partners)
    halo_start(0)

    eye = lax.broadcasted_iota(jnp.int32, (CELLS, CELLS), 0) == lax.broadcasted_iota(jnp.int32, (CELLS, CELLS), 1)
    mask_row = maskv_ref[0:1, :].astype(F32)
    mask_col = jnp.sum(jnp.where(eye, mask_row, 0.0), axis=1, keepdims=True)
    n_mine = jnp.sum(mask_row)
    loads[1].wait()
    ups[...] = (cot_nat[...] * mask_col).astype(BF)
    loads[2].wait()
    chunk = 5 * LANES

    @pl.loop(0, H // chunk)
    def _(i):
        at = pl.multiple_of(i * chunk, chunk)
        actg[:, pl.ds(at, chunk)] = dot(ups[...], wout[pl.ds(at, chunk), :], NT)

    loads[3].wait()
    for b in range(Q):
        start = b * (H // Q) + p * hb
        first, width = window(start, hb, H)
        pick_row = lax.broadcasted_iota(jnp.int32, (LANES, width), 0)
        pick_col = lax.broadcasted_iota(jnp.int32, (LANES, width), 1)
        first = pl.multiple_of(first, LANES)
        pick = ((pick_col == pick_row + (start - first)) & (pick_row < hb)).astype(F32)
        pick_low = pick.astype(BF)
        wo_t[b * LANES : (b + 1) * LANES, :] = dot(pick_low, wout[pl.ds(first, width), :]).astype(BF)
        wi_t[b * LANES : (b + 1) * LANES, :] = dot(pick_low, win[:, pl.ds(first, width)], NT).astype(BF)
        bi_t[b * LANES : (b + 1) * LANES, :] = jnp.sum(pick * bin_ref[:, pl.ds(first, width)], axis=1, keepdims=True)

    def rows_copy(which, src, dst, s):
        at = pl.multiple_of(p * CELLS, 16)
        return remote(src, dst.at[pl.ds(at, CELLS)], rows_send.at[which, s], rows_recv.at[which, s], in_plane(s))

    def rows_start(which, src, dst):
        @pl.loop(1, INNER)
        def _(s):
            rows_copy(which, src, dst, s).start()

        dst[pl.ds(pl.multiple_of(p * CELLS, 16), CELLS), :] = src[...]

    def rows_wait(which, src, dst):
        @pl.loop(1, INNER)
        def _(s):
            rows_copy(which, src, dst, s).wait()

    rows_start(0, ups, uall)

    halo_wait(0)
    fill_pad(0, xc)

    def depthwise(dst, flip):
        @pl.loop(0, TILE_SIDE)
        def _(r):
            acc = [None] * TILE_SIDE
            for a in range(KERNEL):
                base = pl.multiple_of((r + a) * (PAD_SIDE * SUB), SUB)
                row = [pad[pl.ds(base + j * SUB, SUB), :] for j in range(PAD_SIDE)]
                for b in range(KERNEL):
                    tap = a * KERNEL + b
                    if flip:
                        tap = KERNEL * KERNEL - 1 - tap
                    k = kc[tap * SUB : (tap + 1) * SUB, :]
                    for c in range(TILE_SIDE):
                        term = k * row[c + b]
                        acc[c] = term if acc[c] is None else acc[c] + term
            out = pl.multiple_of(r * (TILE_SIDE * SUB), SUB)
            for c in range(TILE_SIDE):
                dst[pl.ds(out + c * SUB, SUB), :] = acc[c]

    depthwise(conv, False)

    def cell_mask(i):
        return mask_ref[0, i].astype(F32)

    def over_cells(fun, init):
        def body(r, carry):
            at = r * TILE_SIDE
            for c in range(TILE_SIDE):
                rows = pl.ds(pl.multiple_of(at * SUB, SUB) + c * SUB, SUB)
                carry = fun(at + c, rows, carry)
            return carry

        return lax.fori_loop(0, TILE_SIDE, body, init)

    zero = jnp.zeros((SUB, LANES), F32)
    my_sum = over_cells(lambda i, rows, acc: acc + conv[rows, :] * cell_mask(i), zero)
    my_mean = my_sum / n_mine

    def deviation(i, rows, acc):
        d = conv[rows, :] - my_mean
        return acc + d * d * cell_mask(i)

    my_dev = over_cells(deviation, zero)
    sub_row = lax.broadcasted_iota(jnp.int32, (SUB, LANES), 0)

    def put_moments(ref, total, dev, count):
        ref[0:SUB, :] = jnp.where(sub_row == SUB - 1, count, total)
        ref[SUB : 2 * SUB, :] = dev

    def vec_exchange(e, src, slots):
        def copy(s):
            return remote(src, slots.at[s], vec_send.at[e, s], vec_recv.at[e, s], in_plane(s))

        @pl.loop(1, INNER)
        def _(s):
            copy(s).start()

        @pl.loop(1, INNER)
        def _(s):
            copy(s).wait()

    def col_exchange(e, src, slots):
        def copy(t):
            return remote(src, slots.at[t], col_send.at[e, t], col_recv.at[e, t], in_column(t))

        @pl.loop(1, Q)
        def _(t):
            copy(t).start()

        @pl.loop(1, Q)
        def _(t):
            copy(t).wait()

    def merge_moments(src, slots, count):
        msgs = [src[...]] + [slots[s] for s in range(1, count)]
        counts = [m[SUB - 1 : SUB, :] for m in msgs]
        total, n = msgs[0][0:SUB], counts[0]
        for m, c in zip(msgs[1:], counts[1:]):
            total, n = total + m[0:SUB], n + c
        mean = total / n
        dev = zero
        for m, c in zip(msgs, counts):
            off = m[0:SUB] / c - mean
            dev = dev + m[SUB : 2 * SUB] + c * off * off
        return total, dev, n, mean

    put_moments(stat_sa.at[0], my_sum, my_dev, n_mine)
    vec_exchange(0, stat_sa.at[0], stat_a.at[0])
    plane_sum, plane_dev, plane_n, _ = merge_moments(stat_sa.at[0], stat_a.at[0], INNER)
    put_moments(stat_sb.at[0], plane_sum, plane_dev, plane_n)
    col_exchange(0, stat_sb.at[0], stat_b.at[0])
    _, all_dev, n_row, mean = merge_moments(stat_sb.at[0], stat_b.at[0], Q)
    inv = lax.rsqrt(all_dev / n_row + EPSILON)
    gain_c = gc[0:SUB, :]
    scale_c = inv * gain_c
    inv_n = 1.0 / n_row

    for t in range(LT):
        v = conv[pl.ds(t, CELLS, stride=SUB), :]
        v = (v - mean[t : t + 1]) * inv[t : t + 1] * gain_c[t : t + 1] + gc[SUB + t : SUB + t + 1, :]
        if t == LT - 1:
            v = v[:, :tail]
        nrm[:, lanes(t)] = v.astype(BF)
    rows_start(1, nrm, nall)

    kg[...] = jnp.zeros_like(kg)
    taps = KERNEL * KERNEL * SUB
    branch[...] = jnp.zeros_like(branch)
    x_rows = CELLS
    ng = cot_nat

    @pl.loop(0, H // chunk)
    def _(i):
        at = pl.multiple_of(i * chunk, chunk)
        cols = pl.ds(at, chunk)
        pre = dot(nrm[...], win[:, cols]) + bin_ref[:, cols]
        half = 0.5 * (1.0 + lax.erf(pre * SQRT_HALF))
        act = (pre * half).astype(BF)
        slope = half + pre * INV_ROOT_TAU * jnp.exp(-0.5 * pre * pre)
        pg = (actg[:, cols] * slope).astype(BF)
        branch[...] += dot(act, wout[cols, :])
        part = dot(pg, win[:, cols], NT)

        @pl.when(i == 0)
        def _():
            ng[...] = part

        @pl.when(i > 0)
        def _():
            ng[...] += part

        bias = jnp.sum(pg.astype(F32), axis=0, keepdims=True)
        for j in range(chunk // LANES):
            kg[pl.ds(taps + i * (chunk // LANES) + j, 1), :] = bias[:, j * LANES : (j + 1) * LANES]

    o_block[...] = (x_nat[...] + branch[...] + bout_ref[...]) * mask_col
    ob = jnp.sum(ups[...].astype(F32), axis=0, keepdims=True)
    bias_rows = -(-(H // LANES) // SUB) * SUB
    for t in range(LT):
        v = ob[:, lanes(t)]
        if t == LT - 1 and tail < LANES:
            v = jnp.concatenate([v, jnp.zeros((1, LANES - tail), F32)], axis=1)
        kg[taps + bias_rows + t : taps + bias_rows + t + 1, :] = v

    cells_from(ngc, lambda t: ng[:, lanes(t)], CELLS)

    def grads(i, rows, carry):
        g = ngc[rows, :]
        return carry[0] + g, carry[1] + g * ((conv[rows, :] - mean) * inv)

    shift_part, gain_part = over_cells(grads, (zero, zero))
    stat_sa[1, 0:SUB, :] = shift_part
    stat_sa[1, SUB : 2 * SUB, :] = gain_part
    vec_exchange(1, stat_sa.at[1], stat_a.at[1])
    tot = stat_sa[1]
    for s in range(1, INNER):
        tot = tot + stat_a[1, s]
    stat_sb[1] = tot
    col_exchange(1, stat_sb.at[1], stat_b.at[1])
    for t in range(1, Q):
        tot = tot + stat_b[1, t]
    shift_grad, gain_grad = tot[0:SUB], tot[SUB : 2 * SUB]
    o_vec[0 : 2 * SUB, :] = tot

    def to_conv_grad(r, _):
        at = r * TILE_SIDE
        for c in range(TILE_SIDE):
            rows = pl.ds(pl.multiple_of(at * SUB, SUB) + c * SUB, SUB)
            scaled = (conv[rows, :] - mean) * inv
            ngc[rows, :] = scale_c * (
                ngc[rows, :] - cell_mask(at + c) * (shift_grad + scaled * gain_grad) * inv_n
            )
        return 0

    lax.fori_loop(0, TILE_SIDE, to_conv_grad, 0)
    make_strips(ngc)
    halo_start(1)

    @pl.loop(0, KERNEL)
    def _(a):
        acc = [zero] * KERNEL
        for r in range(TILE_SIDE):
            base = pl.multiple_of((r + a) * (PAD_SIDE * SUB), SUB)
            row = [pad[pl.ds(base + j * SUB, SUB), :] for j in range(PAD_SIDE)]
            for c in range(TILE_SIDE):
                g = ngc[(r * TILE_SIDE + c) * SUB : (r * TILE_SIDE + c + 1) * SUB, :]
                for b in range(KERNEL):
                    acc[b] = acc[b] + g * row[c + b]
        for b in range(KERNEL):
            at = pl.multiple_of(a * (KERNEL * SUB), SUB)
            kg[pl.ds(at + b * SUB, SUB), :] = acc[b]

    rows_wait(0, ups, uall)
    rows_wait(1, nrm, nall)
    part_rows = 3 * LANES

    @pl.loop(0, INNER * CELLS // part_rows)
    def _(i):
        at = pl.multiple_of(i * part_rows, part_rows)
        rows = pl.ds(at, part_rows)
        pre = dot(wi_t[...], nall[rows, :], NT) + bi_t[...]
        half = 0.5 * (1.0 + lax.erf(pre * SQRT_HALF))
        act_t[:, rows] = (pre * half).astype(BF)
        slope = half + pre * INV_ROOT_TAU * jnp.exp(-0.5 * pre * pre)
        pg_t[:, rows] = (dot(wo_t[...], uall[rows, :], NT) * slope).astype(BF)

    og[...] = dot(act_t[...], uall[...])
    zrows = zo_src.shape[1]
    for b in range(Q):
        zo_src[b] = og[b * LANES : b * LANES + zrows, :].astype(BF)

    def zo_copy(t):
        return remote(zo_src.at[lax.rem(q + t, Q)], zo_dst.at[t], z_send.at[0, t], z_recv.at[0, t], in_column(t))

    def zi_copy(t):
        return remote(zi_src.at[lax.rem(q + t, Q)], zi_dst.at[t], z_send.at[1, t], z_recv.at[1, t], in_column(t))

    @pl.loop(1, Q)
    def _(t):
        zo_copy(t).start()

    ig[...] = dot(pg_t[...], nall[...])
    cq = C // Q
    for b in range(Q):
        zi_src[b] = ig[:, b * cq : (b + 1) * cq].astype(BF)

    @pl.loop(1, Q)
    def _(t):
        zi_copy(t).start()

    halo_wait(1)
    fill_pad(1, ngc)
    depthwise(conv, True)
    for t in range(LT):
        v = conv[pl.ds(t, CELLS, stride=SUB), :]
        if t == LT - 1:
            v = v[:, :tail]
        o_fgrad[:, lanes(t)] = v

    part = kg.shape[0] // INNER

    def ks_copy(s):
        to = lax.rem(p + s, INNER)
        return remote(
            kg.at[pl.ds(pl.multiple_of(to * part, SUB), part)], kg_slot.at[s], ks_send.at[0, s], ks_recv.at[0, s], in_plane(s)
        )

    def kc_copy(t):
        return remote(kg_col.at[0], kg_col.at[t], ks_send.at[1, t], ks_recv.at[1, t], in_column(t))

    def kt_copy(s):
        at = pl.ds(pl.multiple_of(p * part, SUB), part)
        return remote(kg_tot.at[at], kg_tot.at[at], ks_send.at[2, s], ks_recv.at[2, s], in_plane(s))

    def run(lo, hi, copy):
        @pl.loop(lo, hi)
        def _(s):
            copy(s).start()

        @pl.loop(lo, hi)
        def _(s):
            copy(s).wait()

    run(1, INNER, ks_copy)
    mine = pl.ds(pl.multiple_of(p * part, SUB), part)
    tot = kg[mine, :]
    for s in range(1, INNER):
        tot = tot + kg_slot[s]
    kg_col[0] = tot
    run(1, Q, kc_copy)
    for t in range(1, Q):
        tot = tot + kg_col[t]
    kg_tot[mine, :] = tot
    run(1, INNER, kt_copy)
    for t in range(LT):
        o_kgrad[:, lanes(t)] = kg_tot[pl.ds(t, KERNEL * KERNEL, stride=SUB), :][:, : (tail if t == LT - 1 else LANES)]
    o_vec[2 * SUB : 2 * SUB + bias_rows + SUB, :] = kg_tot[taps : taps + bias_rows + SUB, :]

    @pl.loop(1, Q)
    def _(t):
        zo_copy(t).wait()
        zi_copy(t).wait()

    own = og[pl.ds(pl.multiple_of(q * LANES, LANES), zrows), :]
    for t in range(1, Q):
        own = own + zo_dst[t].astype(F32)
    o_wout[...] = own[:hb]

    tr[...] = zi_src[q].astype(F32)
    for t in range(1, Q):
        tr[...] += zi_dst[t].astype(F32)
    flat = tr[...]
    flat = jnp.concatenate([flat, jnp.zeros((flat.shape[0], 2 * LANES - cq), F32)], axis=1)
    flat = flat.T
    for d in range(INNER):
        tr_src[d] = flat[d * cb : d * cb + tr_src.shape[1], :]

    def tr_copy(s):
        to = lax.rem(p + s, INNER)
        return remote(tr_src.at[to], tr_dst.at[p], tr_send.at[s], tr_recv.at[s], in_plane(s))

    @pl.loop(1, INNER)
    def _(s):
        tr_copy(s).start()

    tr_dst[p] = tr_src[p]

    @pl.loop(1, INNER)
    def _(s):
        tr_copy(s).wait()

    pieces = []
    for b in range(Q):
        for d in range(INNER):
            pieces.append(tr_dst[d, :, b * LANES : b * LANES + hb])
    o_win[...] = jnp.concatenate(pieces, axis=1)[:cb]


def run_step(N, fields, cotangent, kernel, norm_gain, norm_shift, weight_in, bias_in, weight_out, bias_out, neighbours, land_mask):
    C = fields.shape[-1]
    H = weight_in.shape[1]
    Q = N // INNER
    hb, cb = H // N, C // N
    LT = -(-C // LANES)
    any_ = pl.BlockSpec(memory_space=pl.ANY)
    vmem = pl.BlockSpec(memory_space=pltpu.VMEM)
    smem = pl.BlockSpec(memory_space=pltpu.SMEM)
    bias_rows = -(-(H // LANES) // SUB) * SUB
    kg_rows = KERNEL * KERNEL * SUB + bias_rows + SUB
    kg_rows = -(-kg_rows // (INNER * SUB)) * INNER * SUB
    zrows = -(-hb // 16) * 16
    V, D = pltpu.VMEM, pltpu.SemaphoreType.DMA
    tr_rows = -(-cb // SUB) * SUB
    outs = (
        jax.ShapeDtypeStruct((CELLS, C), F32),
        jax.ShapeDtypeStruct((CELLS, C), F32),
        jax.ShapeDtypeStruct((KERNEL * KERNEL, C), F32),
        jax.ShapeDtypeStruct((3 * SUB + bias_rows, LANES), F32),
        jax.ShapeDtypeStruct((cb, H), F32),
        jax.ShapeDtypeStruct((hb, C), F32),
    )
    cell = (CELLS * SUB, LANES)
    strip = (EDGE * SUB, LANES)
    scratch = [
        V((CELLS, C), F32),
        V((CELLS, C), F32),
        V((C, H), BF),
        V((H, C), BF),
        V(cell, F32),
        V((PAD_SIDE * PAD_SIDE * SUB, LANES), F32),
        V(cell, F32),
        V(cell, F32),
        V((KERNEL * KERNEL * SUB, LANES), F32),
        V((2 * SUB, LANES), F32),
        V(strip, BF),
        V(strip, BF),
        V(strip, BF),
        V(strip, BF),
        V((2, REACH + 1) + strip, BF),
        V((2, REACH + 1) + strip, BF),
        V((2, 2) + strip, BF),
        V((2, 2) + strip, BF),
        V((2, INNER, 2 * SUB, LANES), F32),
        V((2, Q, 2 * SUB, LANES), F32),
        V((2, 2 * SUB, LANES), F32),
        V((2, 2 * SUB, LANES), F32),
        V((CELLS, C), BF),
        V((CELLS, C), BF),
        V((CELLS, H), F32),
        V((CELLS, C), F32),
        V((INNER * CELLS, C), BF),
        V((INNER * CELLS, C), BF),
        V((Q * LANES, C), BF),
        V((Q * LANES, C), BF),
        V((Q * LANES, 1), F32),
        V((Q * LANES, INNER * CELLS), BF),
        V((Q * LANES, INNER * CELLS), BF),
        V((Q * LANES, C), F32),
        V((Q * LANES, C), F32),
        V((Q, zrows, C), BF),
        V((Q, Q * LANES, C // Q), BF),
        V((Q, zrows, C), BF),
        V((Q, Q * LANES, C // Q), BF),
        V((Q * LANES, C // Q), F32),
        V((INNER, tr_rows, Q * LANES), F32),
        V((INNER, tr_rows, Q * LANES), F32),
        V((kg_rows, LANES), F32),
        V((INNER, kg_rows // INNER, LANES), F32),
        V((Q, kg_rows // INNER, LANES), F32),
        V((kg_rows, LANES), F32),
        D((4,)),
        D((2, 2, REACH + 1)),
        D((2, 2, REACH + 1)),
        D((2, INNER)),
        D((2, INNER)),
        D((2, Q)),
        D((2, Q)),
        D((2, INNER)),
        D((2, INNER)),
        D((2, Q)),
        D((2, Q)),
        D((INNER,)),
        D((INNER,)),
        D((3, max(INNER, Q))),
        D((3, max(INNER, Q))),
    ]
    rows = CELLS
    return pl.pallas_call(
        functools.partial(step_kernel, N, C, H),
        out_shape=outs,
        in_specs=[any_, any_, vmem, vmem, vmem, any_, vmem, any_, vmem, smem, smem, vmem],
        out_specs=[vmem] * len(outs),
        scratch_shapes=scratch,
        compiler_params=pltpu.CompilerParams(
            collective_id=0, has_side_effects=True, vmem_limit_bytes=58 * 1024 * 1024
        ),
        cost_estimate=pl.CostEstimate(
            flops=20 * rows * C * H, bytes_accessed=4 * C * H + 8 * rows * C, transcendentals=4 * rows * H
        ),
        name="step",
    )(
        fields,
        cotangent,
        kernel,
        norm_gain.reshape(1, C),
        norm_shift.reshape(1, C),
        weight_in,
        bias_in.reshape(1, H),
        weight_out,
        bias_out.reshape(1, C),
        neighbours,
        land_mask,
        land_mask,
    )


def local_step(N, grad_shape, fields, cotangent, kernel, norm_gain, norm_shift, weight_in, bias_in, weight_out, bias_out, neighbours, land_mask):
    C = fields.shape[-1]
    H = weight_in.shape[1]
    block, fgrad, kgrad, vec, gwin, gwout = run_step(
        N, fields, cotangent, kernel, norm_gain, norm_shift, weight_in, bias_in, weight_out, bias_out, neighbours, land_mask
    )
    bias_rows = -(-(H // LANES) // SUB) * SUB
    rest = jnp.zeros((fields.shape[0] - 1,) + block.shape, F32)
    return (
        jnp.concatenate([block[None], rest], axis=0),
        jnp.concatenate([(fgrad + cotangent[0] * land_mask[0].astype(F32)[:, None])[None], rest], axis=0),
        kgrad,
        vec[SUB : 2 * SUB].reshape(-1)[:C],
        vec[0:SUB].reshape(-1)[:C],
        gwin.reshape(grad_shape),
        vec[2 * SUB : 2 * SUB + bias_rows].reshape(-1)[:H],
        gwout.reshape(grad_shape),
        vec[2 * SUB + bias_rows : 3 * SUB + bias_rows].reshape(-1)[:C],
    )


def from_behind(shard, axis, by):
    size = lax.axis_size(axis)
    pairs = [(i, i + by) for i in range(size) if 0 <= i + by < size]
    return lax.ppermute(shard, axis, pairs)


def gelu_value(pre):
    return 0.5 * pre * (1.0 + lax.erf(pre * SQRT_HALF))


def gelu_slope(pre):
    return 0.5 * (1.0 + lax.erf(pre * SQRT_HALF)) + pre * INV_ROOT_TAU * jnp.exp(-0.5 * pre * pre)


def pad_tiles(centre, nearby):
    margin = KERNEL // 2
    upper_rows = jnp.concatenate(
        [
            nearby[:, 0, -margin:, -margin:],
            nearby[:, 1, -margin:, :],
            nearby[:, 2, -margin:, :margin],
        ],
        axis=2,
    )
    middle = jnp.concatenate([nearby[:, 3, :, -margin:], centre, nearby[:, 4, :, :margin]], axis=2)
    bottom = jnp.concatenate(
        [nearby[:, 5, :margin, -margin:], nearby[:, 6, :margin, :], nearby[:, 7, :margin, :margin]],
        axis=2,
    )
    return jnp.concatenate([upper_rows, middle, bottom], axis=1)


def depthwise(centre, nearby, kernel):
    padded = pad_tiles(centre, nearby)
    tile_side = centre.shape[1]
    summed = jnp.zeros(centre.shape, jnp.float32)
    for row_tap in range(KERNEL):
        for col_tap in range(KERNEL):
            summed = (
                summed
                + kernel[row_tap * KERNEL + col_tap]
                * padded[:, row_tap : row_tap + tile_side, col_tap : col_tap + tile_side]
            )
    return summed


def feed_both(normed_low, grads_low, weight_in, bias_in, weight_out, bias_out):
    width = normed_low.shape[-1]
    rows = normed_low.reshape(-1, width)
    upstream = grads_low.reshape(-1, width)
    pre = jnp.dot(rows, weight_in, preferred_element_type=jnp.float32) + bias_in
    act_low = gelu_value(pre).astype(jnp.bfloat16)
    branch = jnp.dot(act_low, weight_out, preferred_element_type=jnp.float32) + bias_out
    act_grad = lax.dot_general(
        upstream, weight_out, (((1,), (1,)), ((), ())), preferred_element_type=jnp.float32
    )
    pre_low = (act_grad * gelu_slope(pre)).astype(jnp.bfloat16)
    normed_grad = lax.dot_general(
        pre_low, weight_in, (((1,), (1,)), ((), ())), preferred_element_type=jnp.float32
    )
    in_grad = lax.dot_general(
        rows, pre_low, (((0,), (0,)), ((), ())), preferred_element_type=jnp.float32
    )
    out_grad = lax.dot_general(
        act_low, upstream, (((0,), (0,)), ((), ())), preferred_element_type=jnp.float32
    )
    in_bias = jnp.sum(pre_low, axis=0, dtype=jnp.float32)
    out_bias = jnp.sum(upstream, axis=0, dtype=jnp.float32)
    return (
        branch.reshape(normed_low.shape),
        normed_grad.reshape(normed_low.shape),
        in_grad,
        in_bias,
        out_grad,
        out_bias,
    )


def general(
    fields,
    cotangent,
    kernel,
    norm_gain,
    norm_shift,
    weight_in,
    bias_in,
    weight_out,
    bias_out,
    neighbours,
    land_mask,
):
    position = lax.axis_index("tile")
    devices = lax.axis_size("tile")
    slots = fields.shape[0]
    width = fields.shape[-1]
    ocean = land_mask.astype(jnp.float32)
    cell_weight = ocean[:, :, None]
    arrivals = []
    for offset in range(-REACH, REACH + 1):
        if offset == 0:
            arrivals.append(fields)
        else:
            arrivals.append(from_behind(fields, "tile", -offset))
    stacked = jnp.concatenate(arrivals + [jnp.zeros((1,) + fields.shape[1:], jnp.float32)], axis=0)
    bucket = (2 * REACH + 1) * slots
    source = neighbours // slots - position + REACH
    places = jnp.where(neighbours < 0, bucket, source * slots + neighbours % slots).reshape(-1)
    nearby = jnp.take(stacked, places, axis=0).reshape(slots, 8, TILE_SIDE, TILE_SIDE, width)
    centre = fields.reshape(slots, TILE_SIDE, TILE_SIDE, width)
    conv_tiles, pullback = jax.vjp(depthwise, centre, nearby, kernel)
    conv = conv_tiles.reshape(fields.shape)
    ocean_count, first_sum = lax.psum(
        (jnp.sum(ocean), jnp.sum(conv * cell_weight, axis=(0, 1))), "tile"
    )
    centre_mean = first_sum / ocean_count
    spread = (
        lax.psum(jnp.sum(jnp.square(conv - centre_mean) * cell_weight, axis=(0, 1)), "tile")
        / ocean_count
    )
    inv_spread = lax.rsqrt(spread + EPSILON)
    scaled = (conv - centre_mean) * inv_spread
    normed_low = (scaled * norm_gain + norm_shift).astype(jnp.bfloat16)
    grads_low = (cotangent * cell_weight).astype(jnp.bfloat16)
    branch, normed_grad, in_grad, in_bias, out_grad, out_bias = feed_both(
        normed_low, grads_low, weight_in, bias_in, weight_out, bias_out
    )
    block_out = (fields + branch) * cell_weight
    grad_rows = 8 * devices
    weight_in_grad, weight_out_grad = (
        lax.psum_scatter(in_grad.reshape(grad_rows, -1), "tile", scatter_dimension=0, tiled=True),
        lax.psum_scatter(out_grad.reshape(grad_rows, -1), "tile", scatter_dimension=0, tiled=True),
    )
    shift_part = jnp.sum(normed_grad, axis=(0, 1))
    gain_part = jnp.sum(normed_grad * scaled, axis=(0, 1))
    shift_grad, gain_grad, bias_in_grad, bias_out_grad = lax.psum(
        (shift_part, gain_part, in_bias, out_bias), "tile"
    )
    conv_grad = (
        norm_gain
        * inv_spread
        * (normed_grad - cell_weight * (shift_grad + scaled * gain_grad) / ocean_count)
    )
    centre_grad, nearby_grad, kernel_part = pullback(conv_grad.reshape(centre.shape))
    choose = (places[None, :] == jnp.arange(bucket, dtype=jnp.int32)[:, None]).astype(jnp.float32)
    outgoing = jnp.dot(
        choose, nearby_grad.reshape(slots * 8, -1), precision=lax.Precision.HIGHEST
    ).reshape(2 * REACH + 1, slots, CELLS, width)
    fields_grad = cotangent * cell_weight + centre_grad.reshape(fields.shape) + outgoing[REACH]
    for offset in range(-REACH, REACH + 1):
        if offset != 0:
            fields_grad = fields_grad + from_behind(
                outgoing[offset + REACH].astype(jnp.bfloat16), "tile", offset
            ).astype(jnp.float32)
    kernel_grad = lax.psum(kernel_part, "tile")
    return (
        block_out,
        fields_grad,
        kernel_grad,
        gain_grad,
        shift_grad,
        weight_in_grad,
        bias_in_grad,
        weight_out_grad,
        bias_out_grad,
    )


IN_SPECS = (
    P("tile", None, None),
    P("tile", None, None),
    P(),
    P(),
    P(),
    P(),
    P(),
    P(),
    P(),
    P("tile", None),
    P("tile", None),
)
OUT_SPECS = (
    P("tile", None, None),
    P("tile", None, None),
    P(),
    P(),
    P(),
    P("tile", None),
    P(),
    P("tile", None),
    P(),
)


def solution(mesh):
    N = mesh.shape["tile"]

    def whole(fields, cotangent, kernel, norm_gain, norm_shift, weight_in, *rest):
        C, H = weight_in.shape
        fits = N % INNER == 0 and C % N == 0 and H % N == 0
        if fits:
            body = functools.partial(local_step, N, (SUB, C * H // (SUB * N)))
        else:
            body = general
        return jax.shard_map(body, mesh=mesh, in_specs=IN_SPECS, out_specs=OUT_SPECS, check_vma=False)(
            fields, cotangent, kernel, norm_gain, norm_shift, weight_in, *rest
        )

    return whole
```

```python
import functools
import types

import jax
import jax.numpy as jnp
from jax import lax
from jax.experimental import pallas as pl
from jax.experimental.pallas import tpu as pltpu
from jax.sharding import PartitionSpec as P

TILE_SIDE = 12
KERNEL = 7
CELLS = 144
REACH = 7
MARGIN = KERNEL // 2
PAD_SIDE = TILE_SIDE + 2 * MARGIN
EDGE = MARGIN * TILE_SIDE
TAPS = KERNEL * KERNEL
INNER = 8
CHIPS = INNER // 2
LANES = 128
SUB = 8

EPSILON = 1e-05
SQRT_HALF = 0.7071067811865476
INV_ROOT_TAU = 0.3989422804014327
BF = jnp.bfloat16
F32 = jnp.float32
MESH = pl.DeviceIdType.MESH
NN = (((1,), (0,)), ((), ()))
NT = (((1,), (1,)), ((), ()))


def dot(a, b, dims=NN):
    return lax.dot_general(a, b, dims, preferred_element_type=F32)


def gelu_parts(pre):
    half = 0.5 * (1.0 + lax.erf(pre * SQRT_HALF))
    return pre * half, half + pre * INV_ROOT_TAU * jnp.exp(-0.5 * pre * pre)


def pad_lanes(v, width):
    if v.shape[1] == width:
        return v
    return jnp.concatenate([v, jnp.zeros((v.shape[0], width - v.shape[1]), v.dtype)], axis=1)


class Sizes:
    def __init__(self, N, C, H):
        self.N, self.C, self.H = N, C, H
        self.Q = N // INNER
        self.chips = N // 2
        self.hb, self.cb = H // N, C // N
        self.hq, self.cq = self.hb * self.Q, C // self.Q
        self.LT = -(-C // LANES)
        self.blocks = self.Q + 1
        self.pack_rows = self.hq // self.blocks
        self.pack_lanes = -(-self.blocks * self.cq // LANES) * LANES
        self.bias_rows = -(-(H // LANES) // SUB) * SUB
        rows = TAPS * SUB + self.bias_rows + SUB
        self.kg_rows = -(-rows // (INNER * SUB)) * INNER * SUB
        self.tr_lanes = -(-self.hq // LANES) * LANES
        self.half_rows = CHIPS * CELLS
        self.out_rows = -(-self.hb // SUB) * SUB
        self.in_rows = -(-self.cb // SUB) * SUB

    @staticmethod
    def fits(N, C, H):
        if N % INNER or C % N or H % N or H % (5 * LANES) or C > SUB * LANES or N <= INNER:
            return False
        s = Sizes(N, C, H)
        return s.hq % (16 * s.blocks) == 0 and s.cq <= 2 * LANES and s.hq <= s.Q * LANES


def scratch_of(s):
    V, D = pltpu.VMEM, pltpu.SemaphoreType.DMA
    C, H, Q = s.C, s.H, s.Q
    cell = (CELLS * SUB, LANES)
    strip = (EDGE * SUB, LANES)
    pack = (s.pack_rows, s.pack_lanes)
    return dict(
        x_nat=V((CELLS, C), F32),
        cot_nat=V((CELLS, C), F32),
        win=V((C, H), BF),
        wout=V((C, H), BF),
        xc=V(cell, F32),
        pad=V((PAD_SIDE * PAD_SIDE * SUB, LANES), F32),
        conv=V(cell, F32),
        ngc=V(cell, F32),
        kc=V((TAPS * SUB, LANES), F32),
        gc=V((2 * SUB, LANES), F32),
        strip_top=V(strip, BF),
        strip_bot=V(strip, BF),
        strip_lef=V(strip, BF),
        strip_rig=V(strip, BF),
        from_low=V((2, REACH + 1) + strip, BF),
        from_high=V((2, REACH + 1) + strip, BF),
        from_w=V((2, 2) + strip, BF),
        from_e=V((2, 2) + strip, BF),
        stat_a=V((2, INNER, 2 * SUB, LANES), F32),
        stat_b=V((2, Q, 2 * SUB, LANES), F32),
        stat_sa=V((2, 2 * SUB, LANES), F32),
        stat_sb=V((2, 2 * SUB, LANES), F32),
        nrm=V((CELLS, C), BF),
        dev=V((CELLS, C), BF),
        ups=V((CELLS, C), BF),
        actg=V((CELLS, H), F32),
        branch=V((CELLS, C), F32),
        ng=V((CELLS, C), F32),
        nall=V((2, s.half_rows, C), BF),
        uall=V((2, s.half_rows, C), BF),
        wi_t=V((s.hq, C), BF),
        wo_t=V((s.hq, C), BF),
        bi_t=V((Q * LANES, 1), F32),
        act_t=V((2, s.hq, s.half_rows), BF),
        pg_t=V((2, s.hq, s.half_rows), BF),
        big=V((Q * LANES, C), F32),
        zsrc=V((2, Q) + pack, BF),
        zown=V((2,) + pack, F32),
        zup=V((2, Q) + pack, BF),
        zdn=V((2, Q) + pack, BF),
        tr=V((2 * LANES, s.tr_lanes), F32),
        tr_src=V((INNER, s.in_rows, s.tr_lanes), F32),
        tr_dst=V((INNER, s.in_rows, s.tr_lanes), F32),
        kg=V((s.kg_rows, LANES), F32),
        kg_slot=V((INNER, s.kg_rows // INNER, LANES), F32),
        kg_col=V((Q, s.kg_rows // INNER, LANES), F32),
        kg_tot=V((INNER, s.kg_rows // INNER, LANES), F32),
        tiles=V((max(s.LT * s.out_rows, -(-H // LANES) * s.in_rows), LANES), F32),
        long=V((-(-C * H // (SUB * s.N) // LANES) * SUB, LANES), F32),
        load_sem=D((4,)),
        halo_send=D((2, 2, 9)),
        halo_recv=D((2, 2, REACH + 1)),
        side_send=D((2, 2)),
        side_recv=D((2, 2)),
        vec_send=D((2,)),
        vec_recv=D((2,)),
        col_send=D((2,)),
        col_recv=D((2,)),
        rows_send=D((2, 9)),
        rows_recv=D((2, 9)),
        z_send=D((2, Q)),
        z_up=D((2, Q)),
        z_dn=D((2, Q)),
        tr_send=D((1,)),
        tr_recv=D((1,)),
        ks_send=D((3,)),
        ks_recv=D((3,)),
        out_sem=D((2,)),
    )


def step_kernel(s, names, *refs):
    (
        fields_hbm,
        cot_hbm,
        kernel_ref,
        gain_ref,
        shift_ref,
        win_hbm,
        bin_ref,
        wout_hbm,
        bout_ref,
        nbr_ref,
        mask_ref,
        maskv_ref,
        o_block,
        o_fgrad,
        o_kgrad,
        o_gain,
        o_shift,
        o_win,
        o_bin,
        o_wout,
        o_bout,
    ) = refs[:21]
    m = types.SimpleNamespace(**dict(zip(names, refs[21:], strict=True)))
    N, C, H, Q, hb, cb, LT = s.N, s.C, s.H, s.Q, s.hb, s.cb, s.LT
    hq, cq = s.hq, s.cq
    tail = C - (LT - 1) * LANES
    me = lax.axis_index("tile")
    p = lax.rem(me, INNER)
    q = me // INNER
    chip = me // 2
    core = lax.rem(me, 2)
    j = lax.rem(chip, CHIPS)
    twin = me + 1 - 2 * core

    def remote(src, dst, ssem, rsem, dev):
        return pltpu.make_async_remote_copy(
            src_ref=src, dst_ref=dst, send_sem=ssem, recv_sem=rsem, device_id=(dev,), device_id_type=MESH
        )

    def in_plane(k):
        return q * INNER + lax.rem(p + k, INNER)

    def in_column(t):
        return lax.rem(q + t, Q) * INNER + p

    def lanes(t):
        return slice(t * LANES, min((t + 1) * LANES, C))

    loads = [
        pltpu.make_async_copy(fields_hbm.at[0], m.x_nat, m.load_sem.at[0]),
        pltpu.make_async_copy(cot_hbm.at[0], m.cot_nat, m.load_sem.at[1]),
        pltpu.make_async_copy(wout_hbm, m.wout, m.load_sem.at[2]),
        pltpu.make_async_copy(win_hbm, m.win, m.load_sem.at[3]),
    ]
    loads[0].start()
    barrier = pltpu.get_barrier_semaphore()

    @pl.loop(1, REACH + 1)
    def _(k):
        @pl.when(me + k < N)
        def _():
            pl.semaphore_signal(barrier, inc=1, device_id=(me + k,), device_id_type=MESH)

        @pl.when(me - k >= 0)
        def _():
            pl.semaphore_signal(barrier, inc=1, device_id=(me - k,), device_id_type=MESH)

    @pl.loop(1, Q)
    def _(t):
        pl.semaphore_signal(barrier, inc=1, device_id=(in_column(t),), device_id_type=MESH)

    def cells_from(dst, tile_of, count):
        for t in range(SUB):
            v = pad_lanes(tile_of(t), LANES) if t < LT else jnp.zeros((count, LANES), F32)
            dst[pl.ds(t, count, stride=SUB), :] = v

    cells_from(m.kc, lambda t: kernel_ref[:, lanes(t)], TAPS)
    for t in range(SUB):
        for row, ref in ((0, gain_ref), (1, shift_ref)):
            v = pad_lanes(ref[lanes(t)].reshape(1, -1), LANES) if t < LT else jnp.zeros((1, LANES), F32)
            m.gc[row * SUB + t : row * SUB + t + 1, :] = v

    loads[0].wait()
    for copy in loads[1:]:
        copy.start()
    cells_from(m.xc, lambda t: m.x_nat[:, lanes(t)], CELLS)

    def make_strips(src):
        m.strip_top[...] = src[0 : EDGE * SUB, :].astype(BF)
        m.strip_bot[...] = src[(CELLS - EDGE) * SUB : CELLS * SUB, :].astype(BF)
        lef, rig = [], []
        for r in range(TILE_SIDE):
            row = r * TILE_SIDE * SUB
            lef.append(src[row : row + MARGIN * SUB, :])
            rig.append(src[row + (TILE_SIDE - MARGIN) * SUB : row + TILE_SIDE * SUB, :])
        m.strip_lef[...] = jnp.concatenate(lef, axis=0).astype(BF)
        m.strip_rig[...] = jnp.concatenate(rig, axis=0).astype(BF)

    class Way:
        def __init__(self, e, up):
            self.e, self.up = e, up
            self.sign = 1 if up else -1
            self.strip = m.strip_bot if up else m.strip_top
            self.buf = m.from_low if up else m.from_high
            self.far_core = 1 if up else 0
            self.near_core = 0 if up else 1
            self.w = 0 if up else 1

        def copy(self, src, slot, send, dev):
            return remote(
                src, self.buf.at[self.e, slot], m.halo_send.at[self.e, self.w, send], m.halo_recv.at[self.e, self.w, slot], dev
            )

        def to_there(self, k):
            return (chip + k < s.chips) if self.up else (chip - k >= 0)

        def from_there(self, k):
            return (chip - k >= 0) if self.up else (chip + k < s.chips)

        def direct(self, k):
            return self.copy(self.strip, 2 * k, k, me + self.sign * 2 * k)

        def far(self):
            return self.copy(self.strip, REACH, 4, me + self.sign * REACH)

        def near(self):
            return self.copy(self.strip, 1, 5, twin)

        def slot_at(self, k, its_core):
            return 2 * k - 1 + 2 * its_core if self.up else 2 * k + 1 - 2 * its_core

        def hand(self, k):
            return self.copy(self.buf.at[self.e, 2 * k], self.slot_at(k, 1 - core), 5 + k, twin)

        def handed(self, k):
            return self.copy(self.strip, self.slot_at(k, core), 5 + k, twin)

        def start(self):
            for k in (3, 2, 1):

                @pl.when(self.to_there(k))
                def _(k=k):
                    self.direct(k).start()

            @pl.when(self.to_there(4) & (core == self.far_core))
            def _():
                self.far().start()

            @pl.when(core == self.near_core)
            def _():
                self.near().start()

        def relay(self):
            for k in (1, 2, 3):

                @pl.when(self.from_there(k))
                def _(k=k):
                    self.direct(k).wait_recv()
                    self.hand(k).start()

        def finish(self):
            for k in (1, 2, 3):

                @pl.when(self.from_there(k))
                def _(k=k):
                    self.hand(k).wait_send()
                    self.handed(k).wait_recv()

                @pl.when(self.to_there(k))
                def _(k=k):
                    self.direct(k).wait_send()

            @pl.when(self.to_there(4) & (core == self.far_core))
            def _():
                self.far().wait_send()

            @pl.when(self.from_there(4) & (core != self.far_core))
            def _():
                self.far().wait_recv()

            @pl.when(core == self.near_core)
            def _():
                self.near().wait_send()

            @pl.when(core != self.near_core)
            def _():
                self.near().wait_recv()

    def east(e):
        return remote(m.strip_rig, m.from_w.at[e, 1], m.side_send.at[e, 0], m.side_recv.at[e, 0], me + 1)

    def west(e):
        return remote(m.strip_lef, m.from_e.at[e, 1], m.side_send.at[e, 1], m.side_recv.at[e, 1], me - 1)

    def halo_start(e):
        Way(e, True).start()
        Way(e, False).start()

        @pl.when(me + 1 < N)
        def _():
            east(e).start()

        @pl.when(me >= 1)
        def _():
            west(e).start()

    def halo_relay(e):
        Way(e, True).relay()
        Way(e, False).relay()

    def halo_finish(e):
        Way(e, True).finish()
        Way(e, False).finish()

        @pl.when(me + 1 < N)
        def _():
            east(e).wait_send()
            west(e).wait_recv()

        @pl.when(me >= 1)
        def _():
            west(e).wait_send()
            east(e).wait_recv()

    zero_strip = jnp.zeros((EDGE * SUB, LANES), BF)
    for e in range(2):
        m.from_low[e, 0] = zero_strip
        m.from_high[e, 0] = zero_strip
        m.from_w[e, 0] = zero_strip
        m.from_e[e, 0] = zero_strip

    def fill_pad(e, centre):
        def low_slot(d):
            n = nbr_ref[0, d]
            return jnp.clip(jnp.where(n < 0, 0, me - lax.shift_right_arithmetic(n, 1)), 0, REACH)

        def high_slot(d):
            n = nbr_ref[0, d]
            return jnp.clip(jnp.where(n < 0, 0, lax.shift_right_arithmetic(n, 1) - me), 0, REACH)

        def there(d):
            return jnp.where(nbr_ref[0, d] < 0, 0, 1)

        def put(row, col, value):
            at = (row * PAD_SIDE + col) * SUB
            m.pad[at : at + value.shape[0], :] = value

        S, M, T = SUB, MARGIN, TILE_SIDE
        for buf, slot, dirs, row0 in ((m.from_low, low_slot, (0, 1, 2), 0), (m.from_high, high_slot, (5, 6, 7), M + T)):
            left = buf[e, slot(dirs[0])].astype(F32)
            mid = buf[e, slot(dirs[1])].astype(F32)
            right = buf[e, slot(dirs[2])].astype(F32)
            for r in range(M):
                at = r * T * S
                put(row0 + r, 0, left[at + (T - M) * S : at + T * S])
                put(row0 + r, M, mid[at : at + T * S])
                put(row0 + r, M + T, right[at : at + M * S])
        from_west = m.from_w[e, there(3)].astype(F32)
        from_east = m.from_e[e, there(4)].astype(F32)
        for r in range(T):
            put(M + r, 0, from_west[r * M * S : (r + 1) * M * S])
            put(M + r, M, centre[r * T * S : (r + 1) * T * S, :])
            put(M + r, M + T, from_east[r * M * S : (r + 1) * M * S])

    make_strips(m.xc)
    n_partners = jnp.minimum(REACH, N - 1 - me) + jnp.minimum(REACH, me) + (Q - 1)
    pl.semaphore_wait(barrier, n_partners)
    halo_start(0)

    eye = lax.broadcasted_iota(jnp.int32, (CELLS, CELLS), 0) == lax.broadcasted_iota(jnp.int32, (CELLS, CELLS), 1)
    mask_row = maskv_ref[0:1, :].astype(F32)
    mask_col = jnp.sum(jnp.where(eye, mask_row, 0.0), axis=1, keepdims=True)
    n_mine = jnp.sum(mask_row)
    loads[1].wait()
    m.ups[...] = (m.cot_nat[...] * mask_col).astype(BF)
    across_x = j + 1 - 2 * lax.rem(j, 2)
    across_y = lax.rem(j + 2, CHIPS)
    across = CHIPS - 1 - j
    dev_x = q * INNER + 2 * across_x + core
    dev_y = q * INNER + 2 * across_y + core
    part_a = (0, 5 * 16)
    part_b = (5 * 16, CELLS)
    every = (0, CELLS)

    class Rows:
        def __init__(self, which, src, dst):
            self.which, self.src, self.dst = which, src, dst

        def at(self, jj, cc, part):
            return self.dst.at[cc, pl.ds(pl.multiple_of(jj * CELLS + part[0], 16), part[1] - part[0])]

        def copy(self, sem, src, jj, cc, part, dev):
            return remote(src, self.at(jj, cc, part), m.rows_send.at[self.which, sem], m.rows_recv.at[self.which, sem], dev)

        def sends(self):
            own = [(0, self.src, j, every, dev_x), (1, self.src, j, every, dev_y), (4, self.src, j, every, twin)]
            for sem, jj, part, dev in (
                (2, across_x, part_a, dev_y),
                (3, across_y, part_b, dev_x),
                (5, across_x, every, twin),
                (6, across_y, every, twin),
                (7, across, part_a, twin),
                (8, across, part_b, twin),
            ):
                own.append((sem, self.at(jj, core, part), jj, part, dev))
            return {o[0]: functools.partial(self.copy, o[0], o[1], o[2], core, o[3], o[4]) for o in own}

        def arrivals(self):
            return {
                sem: functools.partial(self.copy, sem, self.at(jj, cc, part), jj, cc, part, twin)
                for sem, jj, cc, part in (
                    (0, across_x, core, every),
                    (1, across_y, core, every),
                    (2, across, core, part_a),
                    (3, across, core, part_b),
                    (4, j, 1 - core, every),
                    (5, across_x, 1 - core, every),
                    (6, across_y, 1 - core, every),
                    (7, across, 1 - core, part_a),
                    (8, across, 1 - core, part_b),
                )
            }

        def start(self):
            for sem in (0, 1, 4):
                self.sends()[sem]().start()
            self.dst[core, pl.ds(pl.multiple_of(j * CELLS, 16), CELLS), :] = self.src[...]

        def relay(self):
            for came, then in ((0, (2, 5)), (1, (3, 6))):
                self.arrivals()[came]().wait_recv()
                for sem in then:
                    self.sends()[sem]().start()

        def relay_across(self):
            for came, then in ((2, 7), (3, 8)):
                self.arrivals()[came]().wait_recv()
                self.sends()[then]().start()

        def finish(self):
            for sem in range(4, 9):
                self.arrivals()[sem]().wait_recv()
            for sem in range(9):
                self.sends()[sem]().wait_send()

    ups_rows = Rows(0, m.ups, m.uall)
    dev_rows = Rows(1, m.dev, m.nall)
    halo_relay(0)
    ups_rows.start()
    halo_finish(0)
    fill_pad(0, m.xc)

    def depthwise(dst, flip):
        @pl.loop(0, TILE_SIDE)
        def _(r):
            acc = [None] * TILE_SIDE
            for a in range(KERNEL):
                base = pl.multiple_of((r + a) * (PAD_SIDE * SUB), SUB)
                row = [m.pad[pl.ds(base + i * SUB, SUB), :] for i in range(PAD_SIDE)]
                for b in range(KERNEL):
                    tap = a * KERNEL + b
                    if flip:
                        tap = TAPS - 1 - tap
                    k = m.kc[tap * SUB : (tap + 1) * SUB, :]
                    for c in range(TILE_SIDE):
                        term = k * row[c + b]
                        acc[c] = term if acc[c] is None else acc[c] + term
            out = pl.multiple_of(r * (TILE_SIDE * SUB), SUB)
            for c in range(TILE_SIDE):
                dst[pl.ds(out + c * SUB, SUB), :] = acc[c]

    depthwise(m.conv, False)

    def cell_mask(i):
        return mask_ref[0, i].astype(F32)

    def over_cells(fun, init):
        def body(r, carry):
            at = r * TILE_SIDE
            for c in range(TILE_SIDE):
                rows = pl.ds(pl.multiple_of(at * SUB, SUB) + c * SUB, SUB)
                carry = fun(at + c, rows, carry)
            return carry

        return lax.fori_loop(0, TILE_SIDE, body, init)

    zero = jnp.zeros((SUB, LANES), F32)
    my_sum = over_cells(lambda i, rows, acc: acc + m.conv[rows, :] * cell_mask(i), zero)
    my_mean = my_sum / n_mine

    def deviation(i, rows, acc):
        d = m.conv[rows, :] - my_mean
        return acc + d * d * cell_mask(i)

    my_dev = over_cells(deviation, zero)
    sub_row = lax.broadcasted_iota(jnp.int32, (SUB, LANES), 0)

    def put_moments(ref, total, dev, count):
        ref[0:SUB, :] = jnp.where(sub_row == SUB - 1, count, total)
        ref[SUB : 2 * SUB, :] = dev

    def run(lo, hi, copy):
        @pl.loop(lo, hi)
        def _(k):
            copy(k).start()

        @pl.loop(lo, hi)
        def _(k):
            copy(k).wait()

    class Spread:
        def __init__(self, src, slots, send, recv, count, dev):
            self.src, self.slots, self.send, self.recv, self.count, self.dev = src, slots, send, recv, count, dev

        def start(self):
            for k in range(1, self.count):
                remote(self.src, self.slots.at[k], self.send, self.recv, self.dev(k)).start()

        def finish(self):
            whole = self.slots.at[1 : self.count]
            copy = remote(whole, whole, self.send, self.recv, twin)
            copy.wait_send()
            copy.wait_recv()

    def in_planes(e):
        return Spread(m.stat_sa.at[e], m.stat_a.at[e], m.vec_send.at[e], m.vec_recv.at[e], INNER, in_plane)

    def in_columns(e):
        return Spread(m.stat_sb.at[e], m.stat_b.at[e], m.col_send.at[e], m.col_recv.at[e], Q, in_column)

    def merge_moments(msgs):
        counts = [v[SUB - 1 : SUB, :] for v in msgs]
        total, n = msgs[0][0:SUB], counts[0]
        for v, c in zip(msgs[1:], counts[1:]):
            total, n = total + v[0:SUB], n + c
        mean = total / n
        dev = zero
        for v, c in zip(msgs, counts):
            off = v[0:SUB] / c - mean
            dev = dev + v[SUB : 2 * SUB] + c * off * off
        return total, dev, n, mean

    put_moments(m.stat_sa.at[0], my_sum, my_dev, n_mine)
    in_planes(0).start()
    for t in range(LT):
        v = m.conv[pl.ds(t, CELLS, stride=SUB), :] - my_mean[t : t + 1]
        m.dev[:, lanes(t)] = (v[:, :tail] if t == LT - 1 else v).astype(BF)
    dev_rows.start()

    loads[2].wait()
    chunk = 5 * LANES

    @pl.loop(0, H // chunk)
    def _(i):
        cols = pl.ds(pl.multiple_of(i * chunk, chunk), chunk)
        m.actg[:, cols] = dot(m.ups[...], m.wout[:, cols])

    in_planes(0).finish()
    plane_sum, plane_dev, plane_n, _ = merge_moments([m.stat_sa[0]] + [m.stat_a[0, k] for k in range(1, INNER)])
    put_moments(m.stat_sb.at[0], plane_sum, plane_dev, plane_n)
    in_columns(0).start()
    ups_rows.relay()
    loads[3].wait()
    width = min(2 * LANES, H)
    for weight, dst in ((m.win, m.wi_t), (m.wout, m.wo_t)):
        for b in range(Q):
            start = b * (H // Q) + p * hb
            first = pl.multiple_of(jnp.minimum((start // LANES) * LANES, H - width), LANES)
            pick_row = lax.broadcasted_iota(jnp.int32, (LANES, width), 0)
            pick_col = lax.broadcasted_iota(jnp.int32, (LANES, width), 1)
            pick = ((pick_col == pick_row + (start - first)) & (pick_row < hb)).astype(F32)
            m.big[b * hb : b * hb + LANES, :] = dot(pick.astype(BF), weight[:, pl.ds(first, width)], NT)
            if dst is m.wi_t:
                row = bin_ref[pl.ds(first, width)].reshape(1, width)
                m.bi_t[b * hb : b * hb + LANES, :] = jnp.sum(pick * row, axis=1, keepdims=True)
        dst[...] = m.big[0:hq, :].astype(BF)

    in_columns(0).finish()
    _, all_dev, n_row, mean = merge_moments([m.stat_sb[0]] + [m.stat_b[0, t] for t in range(1, Q)])
    inv = lax.rsqrt(all_dev / n_row + EPSILON)
    gain_c = m.gc[0:SUB, :]
    shift_c = m.gc[SUB : 2 * SUB, :]
    scale_c = inv * gain_c
    inv_n = 1.0 / n_row

    for t in range(LT):
        v = m.conv[pl.ds(t, CELLS, stride=SUB), :]
        v = (v - mean[t : t + 1]) * inv[t : t + 1] * gain_c[t : t + 1] + shift_c[t : t + 1]
        m.nrm[:, lanes(t)] = (v[:, :tail] if t == LT - 1 else v).astype(BF)

    m.kg[...] = jnp.zeros_like(m.kg)
    m.branch[...] = jnp.zeros_like(m.branch)
    m.ng[...] = jnp.zeros_like(m.ng)

    def pointwise(i, _):
        at = pl.multiple_of(i * chunk, chunk)
        cols = pl.ds(at, chunk)
        pre = dot(m.nrm[...], m.win[:, cols]) + bin_ref[cols].reshape(1, chunk)
        act, slope = gelu_parts(pre)
        pg = (m.actg[:, cols] * slope).astype(BF)
        m.branch[...] += dot(act.astype(BF), m.wout[:, cols], NT)
        m.ng[...] += dot(pg, m.win[:, cols], NT)
        bias = jnp.sum(pg.astype(F32), axis=0, keepdims=True)
        for k in range(chunk // LANES):
            m.kg[pl.ds(TAPS * SUB + i * (chunk // LANES) + k, 1), :] = bias[:, k * LANES : (k + 1) * LANES]
        return 0

    half_way = H // chunk // 2
    lax.fori_loop(0, half_way, pointwise, 0)
    ups_rows.relay_across()
    dev_rows.relay()
    lax.fori_loop(half_way, H // chunk, pointwise, 0)

    cells_from(m.ngc, lambda t: m.ng[:, lanes(t)], CELLS)

    def grads(i, rows, carry):
        g = m.ngc[rows, :]
        return carry[0] + g, carry[1] + g * ((m.conv[rows, :] - mean) * inv)

    shift_part, gain_part = over_cells(grads, (zero, zero))
    m.stat_sa[1, 0:SUB, :] = shift_part
    m.stat_sa[1, SUB : 2 * SUB, :] = gain_part
    in_planes(1).start()
    dev_rows.relay_across()
    m.branch[...] = (m.x_nat[...] + m.branch[...] + bout_ref[...].reshape(1, C)) * mask_col
    out_block = pltpu.make_async_copy(m.branch, o_block, m.out_sem.at[0])
    out_block.start()
    bias = jnp.sum(m.ups[...].astype(F32), axis=0, keepdims=True)
    for t in range(LT):
        at = TAPS * SUB + s.bias_rows + t
        m.kg[at : at + 1, :] = pad_lanes(bias[:, lanes(t)], LANES)

    in_planes(1).finish()
    tot = m.stat_sa[1]
    for k in range(1, INNER):
        tot = tot + m.stat_a[1, k]
    m.stat_sb[1] = tot
    in_columns(1).start()
    ups_rows.finish()
    dev_rows.finish()
    for k in range(1, INNER):
        pk = lax.rem(p + INNER - k, INNER)
        rows = pl.ds(pl.multiple_of((pk // 2) * CELLS, 16), CELLS)
        cc = lax.rem(pk, 2)
        its = m.stat_a[0, k]
        off = (its[0:SUB] / its[SUB - 1 : SUB] - mean) * scale_c + shift_c
        for t in range(LT):
            w = lanes(t).stop - lanes(t).start
            v = m.nall[cc, rows, lanes(t)].astype(F32)
            m.nall[cc, rows, lanes(t)] = (v * scale_c[t : t + 1, :w] + off[t : t + 1, :w]).astype(BF)
    m.nall[core, pl.ds(pl.multiple_of(j * CELLS, 16), CELLS), :] = m.nrm[...]
    for cc in (core, 1 - core):
        for lo, hi in ((0, 2 * LANES), (2 * LANES, s.half_rows)):
            pre = dot(m.wi_t[...], m.nall[cc, lo:hi, :], NT) + m.bi_t[0:hq, :]
            act, slope = gelu_parts(pre)
            m.act_t[cc, :, lo:hi] = act.astype(BF)
            m.pg_t[cc, :, lo:hi] = (dot(m.wo_t[...], m.uall[cc, lo:hi, :], NT) * slope).astype(BF)

    def keep_rows(value, rows):
        for t in range(-(-value.shape[1] // LANES)):
            m.tiles[t * rows : (t + 1) * rows, :] = pad_lanes(value[:, t * LANES : (t + 1) * LANES], LANES)

    def lay_out(rows, count, width, dst):
        long = count * width // SUB
        tiles = -(-width // LANES)
        groups = {}
        for r in range(SUB):
            groups.setdefault(r * long % width, []).append(r)
        for off, rs in groups.items():
            first = [r * long // width for r in rs]
            n = len(rs)
            step = first[1] - first[0] if n > 1 else 1
            assert all(f == first[0] + i * step for i, f in enumerate(first))
            pieces, row, at, left = [], first[0], off, long
            while left:
                w = min(left, width - at)
                for t in range(at // LANES, -(-(at + w) // LANES)):
                    lo, hi = max(at, t * LANES), min(at + w, (t + 1) * LANES)
                    where = pl.ds(t * rows + row, n, stride=step) if n > 1 else pl.ds(t * rows + row, 1)
                    pieces.append(m.tiles[where, :][:, lo - t * LANES : hi - t * LANES])
                row, at, left = row + 1, 0, left - w
            v = jnp.concatenate(pieces, axis=1)
            for t in range(-(-long // LANES)):
                w = min(LANES, long - t * LANES)
                where = pl.ds(t * SUB + rs[0], n, stride=rs[1] - rs[0]) if n > 1 else pl.ds(t * SUB + rs[0], 1)
                m.long[where, :] = pad_lanes(v[:, t * LANES : t * LANES + w], LANES)
        for t in range(-(-long // LANES)):
            w = min(LANES, long - t * LANES)
            dst[:, t * LANES : t * LANES + w] = m.long[t * SUB : (t + 1) * SUB, :][:, :w]

    in_columns(1).finish()
    for t in range(1, Q):
        tot = tot + m.stat_b[1, t]
    shift_grad, gain_grad = tot[0:SUB], tot[SUB : 2 * SUB]

    def to_conv_grad(r, _):
        at = r * TILE_SIDE
        for c in range(TILE_SIDE):
            rows = pl.ds(pl.multiple_of(at * SUB, SUB) + c * SUB, SUB)
            scaled = (m.conv[rows, :] - mean) * inv
            m.ngc[rows, :] = scale_c * (
                m.ngc[rows, :] - cell_mask(at + c) * (shift_grad + scaled * gain_grad) * inv_n
            )
        return 0

    lax.fori_loop(0, TILE_SIDE, to_conv_grad, 0)
    make_strips(m.ngc)
    halo_start(1)

    nb, pr, width_in = s.blocks, s.pack_rows, s.blocks * cq

    def pack_in(b):
        cols = slice(b * cq, (b + 1) * cq)
        return pad_lanes(jnp.concatenate([m.big[i * pr : (i + 1) * pr, cols] for i in range(nb)], axis=1), s.pack_lanes)

    def pack_out(b):
        top = m.big[b * hb : b * hb + pr, :]
        rest = m.big[b * hb + pr : (b + 1) * hb, :]
        side = jnp.concatenate([rest[:, g * cq : (g + 1) * cq] for g in range(Q)], axis=0)
        return pad_lanes(jnp.concatenate([top, side], axis=1), s.pack_lanes)

    def z_up(kind, b):
        return remote(m.zsrc.at[kind, b], m.zup.at[kind, b], m.z_send.at[kind, b], m.z_up.at[kind, b], me + INNER)

    def z_dn(kind, b):
        return remote(m.zsrc.at[kind, b], m.zdn.at[kind, b], m.z_send.at[kind, b], m.z_dn.at[kind, b], me - INNER)

    def z_add(kind, b, buf):
        m.zsrc[kind, b] = (m.zsrc[kind, b].astype(F32) + buf[kind, b].astype(F32)).astype(BF)

    def z_hop(kind, hop):
        @pl.when(q == hop)
        def _():
            for b in range(Q - 1, hop, -1):
                if hop > 0:
                    z_up(kind, b).wait_recv()
                    z_add(kind, b, m.zup)
                z_up(kind, b).start()

        @pl.when(q == Q - 1 - hop)
        def _():
            for b in range(0, Q - 1 - hop):
                if hop > 0:
                    z_dn(kind, b).wait_recv()
                    z_add(kind, b, m.zdn)
                z_dn(kind, b).start()

    def z_total(kind):
        for b in range(Q):

            @pl.when(q > b)
            def _(b=b):
                z_dn(kind, b).wait_send()

            @pl.when(q < b)
            def _(b=b):
                z_up(kind, b).wait_send()

        @pl.when(q > 0)
        def _():
            z_up(kind, q).wait_recv()

        @pl.when(q < Q - 1)
        def _():
            z_dn(kind, q).wait_recv()

        low = jnp.where(q > 0, m.zup[kind, q].astype(F32), 0.0)
        high = jnp.where(q < Q - 1, m.zdn[kind, q].astype(F32), 0.0)
        return m.zown[kind] + low + high

    def keep_packed(kind, pack):
        for b in range(Q):
            v = pack(b)
            m.zsrc[kind, b] = v.astype(BF)

            @pl.when(q == b)
            def _(v=v):
                m.zown[kind] = v

    def product(a, rows):
        m.big[0:hq, :] = dot(a[0], rows[0]) + dot(a[1], rows[1])

    product(m.pg_t, m.nall)
    keep_packed(0, pack_in)
    z_hop(0, 0)
    product(m.act_t, m.uall)
    keep_packed(1, pack_out)
    z_hop(1, 0)
    @pl.loop(0, KERNEL)
    def _(a):
        acc = [zero] * KERNEL
        for r in range(TILE_SIDE):
            base = pl.multiple_of((r + a) * (PAD_SIDE * SUB), SUB)
            row = [m.pad[pl.ds(base + i * SUB, SUB), :] for i in range(PAD_SIDE)]
            for c in range(TILE_SIDE):
                g = m.ngc[(r * TILE_SIDE + c) * SUB : (r * TILE_SIDE + c + 1) * SUB, :]
                for b in range(KERNEL):
                    acc[b] = acc[b] + g * row[c + b]
        for b in range(KERNEL):
            m.kg[pl.ds(pl.multiple_of(a * (KERNEL * SUB), SUB) + b * SUB, SUB), :] = acc[b]

    part = s.kg_rows // INNER
    mine = pl.ds(pl.multiple_of(p * part, SUB), part)

    def part_of(k):
        return pl.ds(pl.multiple_of(k * part, SUB), part)

    for k in range(1, INNER):
        remote(m.kg.at[part_of(lax.rem(p + k, INNER))], m.kg_slot.at[k], m.ks_send.at[0], m.ks_recv.at[0], in_plane(k)).start()

    column_sum = Spread(m.kg_col.at[0], m.kg_col, m.ks_send.at[1], m.ks_recv.at[1], Q, in_column)

    z_hop(0, 1)
    halo_relay(1)
    halo_finish(1)
    fill_pad(1, m.ngc)
    depthwise(m.conv, True)
    for t in range(LT):
        v = m.conv[pl.ds(t, CELLS, stride=SUB), :]
        m.ng[:, lanes(t)] = v[:, :tail] if t == LT - 1 else v
    m.ng[...] += m.cot_nat[...] * mask_col
    out_fgrad = pltpu.make_async_copy(m.ng, o_fgrad, m.out_sem.at[1])
    out_fgrad.start()

    whole = m.kg_slot.at[1:INNER]
    copy = remote(whole, whole, m.ks_send.at[0], m.ks_recv.at[0], twin)
    copy.wait_send()
    copy.wait_recv()
    part_sum = m.kg[mine, :]
    for k in range(1, INNER):
        part_sum = part_sum + m.kg_slot[k]
    m.kg_col[0] = part_sum
    column_sum.start()
    for hop in range(2, Q - 1):
        z_hop(0, hop)
    column_sum.finish()
    for t in range(1, Q):
        part_sum = part_sum + m.kg_col[t]
    m.kg_tot[p] = part_sum
    for k in range(1, INNER):
        remote(m.kg_tot.at[p], m.kg_tot.at[p], m.ks_send.at[2], m.ks_recv.at[2], in_plane(k)).start()

    total = z_total(0)
    flat = jnp.concatenate([total[:, i * cq : (i + 1) * cq] for i in range(nb)], axis=0)
    flat = jnp.concatenate([flat, jnp.zeros((s.tr_lanes - hq, cq), F32)], axis=0)
    m.tr[...] = pad_lanes(flat, 2 * LANES).T
    for d in range(INNER):
        m.tr_src[d] = m.tr[d * cb : d * cb + s.in_rows, :]

    for k in range(1, INNER):
        remote(m.tr_src.at[lax.rem(p + k, INNER)], m.tr_dst.at[p], m.tr_send.at[0], m.tr_recv.at[0], in_plane(k)).start()
    m.tr_dst[p] = m.tr_src[p]
    z_hop(1, 1)

    whole = m.kg_tot.at[1:INNER]
    copy = remote(whole, whole, m.ks_send.at[2], m.ks_recv.at[2], twin)
    copy.wait_send()
    copy.wait_recv()

    m.kg[...] = jnp.concatenate([m.kg_tot[k] for k in range(INNER)], axis=0)
    for t in range(LT):
        v = m.kg[pl.ds(t, TAPS, stride=SUB), :]
        o_kgrad[:, lanes(t)] = v[:, :tail] if t == LT - 1 else v

    def to_vector(ref, row, length):
        for t in range(-(-length // LANES)):
            w = min(LANES, length - t * LANES)
            ref[t * LANES : t * LANES + w] = m.kg[row + t, :][:w]

    to_vector(o_bin, TAPS * SUB, H)
    to_vector(o_bout, TAPS * SUB + s.bias_rows, C)
    m.kg[0:SUB, :] = shift_grad
    m.kg[SUB : 2 * SUB, :] = gain_grad
    to_vector(o_shift, 0, C)
    to_vector(o_gain, SUB, C)

    copy = remote(m.tr_dst.at[1:INNER], m.tr_dst.at[1:INNER], m.tr_send.at[0], m.tr_recv.at[0], twin)
    copy.wait_send()
    copy.wait_recv()
    pieces = []
    for b in range(Q):
        for d in range(INNER):
            pieces.append(m.tr_dst[d][:, b * hb : (b + 1) * hb])
    keep_rows(jnp.concatenate(pieces, axis=1)[: s.in_rows], s.in_rows)
    lay_out(s.in_rows, cb, H, o_win)
    for hop in range(2, Q - 1):
        z_hop(1, hop)

    total = z_total(1)
    side = total[:, C:width_in]
    rest = hb - pr
    side = jnp.concatenate([side[g * rest : (g + 1) * rest] for g in range(Q)], axis=1)
    spare = jnp.zeros((s.out_rows - hb, C), F32)
    keep_rows(jnp.concatenate([total[:, :C], side, spare], axis=0), s.out_rows)
    lay_out(s.out_rows, hb, C, o_wout)
    out_block.wait()
    out_fgrad.wait()


def run_step(s, fields, cotangent, kernel, norm_gain, norm_shift, weight_in, bias_in, weight_out, bias_out, neighbours, land_mask):
    C, H = s.C, s.H
    any_ = pl.BlockSpec(memory_space=pl.ANY)
    vmem = pl.BlockSpec(memory_space=pltpu.VMEM)
    smem = pl.BlockSpec(memory_space=pltpu.SMEM)
    long = (SUB, C * H // (SUB * s.N))
    shapes = ((CELLS, C), (CELLS, C), (TAPS, C), (C,), (C,), long, (H,), long, (C,))
    outs = [jax.ShapeDtypeStruct(shape, F32) for shape in shapes]
    scratch = scratch_of(s)
    return pl.pallas_call(
        functools.partial(step_kernel, s, tuple(scratch)),
        out_shape=outs,
        in_specs=[any_, any_, vmem, vmem, vmem, any_, vmem, any_, vmem, smem, smem, vmem],
        out_specs=[any_, any_] + [vmem] * 7,
        scratch_shapes=list(scratch.values()),
        compiler_params=pltpu.CompilerParams(
            collective_id=0, has_side_effects=True, vmem_limit_bytes=58 * 1024 * 1024
        ),
        cost_estimate=pl.CostEstimate(
            flops=20 * CELLS * C * H, bytes_accessed=4 * C * H + 8 * CELLS * C, transcendentals=4 * CELLS * H
        ),
        name="step",
    )(
        fields,
        cotangent,
        kernel,
        norm_gain,
        norm_shift,
        weight_in,
        bias_in,
        weight_out.T,
        bias_out,
        neighbours,
        land_mask,
        land_mask,
    )


def finish_kernel(count, *refs):
    ins, outs, zeros = refs[:count], refs[count : 2 * count], refs[2 * count]
    held, sems, out_sems = refs[2 * count + 1 : 3 * count + 1], refs[3 * count + 1], refs[3 * count + 2]
    into = [pltpu.make_async_copy(src, dst, sems.at[i]) for i, (src, dst) in enumerate(zip(ins, held))]
    for copy in into:
        copy.start()
    zeros[...] = jnp.zeros_like(zeros)
    out = [pltpu.make_async_copy(zeros, outs[i].at[1], out_sems.at[count + i]) for i in range(2)]
    for copy in out:
        copy.start()
    for i in range(count):
        into[i].wait()
        out.append(pltpu.make_async_copy(held[i], outs[i].at[0] if i < 2 else outs[i], out_sems.at[i]))
        out[-1].start()
    for copy in out:
        copy.wait()


def local_step(s, fields, *rest):
    parts = run_step(s, fields, *rest)
    count = len(parts)
    any_ = pl.BlockSpec(memory_space=pl.ANY)
    outs = [jax.ShapeDtypeStruct(fields.shape if i < 2 else v.shape, F32) for i, v in enumerate(parts)]
    held = [pltpu.VMEM(v.shape, F32) for v in parts]
    return tuple(
        pl.pallas_call(
            functools.partial(finish_kernel, count),
            out_shape=outs,
            in_specs=[any_] * count,
            out_specs=[any_] * count,
            scratch_shapes=[pltpu.VMEM((CELLS, s.C), F32)]
            + held
            + [pltpu.SemaphoreType.DMA((count,)), pltpu.SemaphoreType.DMA((count + 2,))],
            name="finish",
        )(*parts)
    )


def from_behind(shard, axis, by):
    size = lax.axis_size(axis)
    pairs = [(i, i + by) for i in range(size) if 0 <= i + by < size]
    return lax.ppermute(shard, axis, pairs)


def gelu_value(pre):
    return 0.5 * pre * (1.0 + lax.erf(pre * SQRT_HALF))


def gelu_slope(pre):
    return 0.5 * (1.0 + lax.erf(pre * SQRT_HALF)) + pre * INV_ROOT_TAU * jnp.exp(-0.5 * pre * pre)


def pad_tiles(centre, nearby):
    margin = KERNEL // 2
    upper_rows = jnp.concatenate(
        [
            nearby[:, 0, -margin:, -margin:],
            nearby[:, 1, -margin:, :],
            nearby[:, 2, -margin:, :margin],
        ],
        axis=2,
    )
    middle = jnp.concatenate([nearby[:, 3, :, -margin:], centre, nearby[:, 4, :, :margin]], axis=2)
    bottom = jnp.concatenate(
        [nearby[:, 5, :margin, -margin:], nearby[:, 6, :margin, :], nearby[:, 7, :margin, :margin]],
        axis=2,
    )
    return jnp.concatenate([upper_rows, middle, bottom], axis=1)


def depthwise(centre, nearby, kernel):
    padded = pad_tiles(centre, nearby)
    tile_side = centre.shape[1]
    summed = jnp.zeros(centre.shape, jnp.float32)
    for row_tap in range(KERNEL):
        for col_tap in range(KERNEL):
            summed = (
                summed
                + kernel[row_tap * KERNEL + col_tap]
                * padded[:, row_tap : row_tap + tile_side, col_tap : col_tap + tile_side]
            )
    return summed


def feed_both(normed_low, grads_low, weight_in, bias_in, weight_out, bias_out):
    width = normed_low.shape[-1]
    rows = normed_low.reshape(-1, width)
    upstream = grads_low.reshape(-1, width)
    pre = jnp.dot(rows, weight_in, preferred_element_type=jnp.float32) + bias_in
    act_low = gelu_value(pre).astype(jnp.bfloat16)
    branch = jnp.dot(act_low, weight_out, preferred_element_type=jnp.float32) + bias_out
    act_grad = lax.dot_general(
        upstream, weight_out, (((1,), (1,)), ((), ())), preferred_element_type=jnp.float32
    )
    pre_low = (act_grad * gelu_slope(pre)).astype(jnp.bfloat16)
    normed_grad = lax.dot_general(
        pre_low, weight_in, (((1,), (1,)), ((), ())), preferred_element_type=jnp.float32
    )
    in_grad = lax.dot_general(
        rows, pre_low, (((0,), (0,)), ((), ())), preferred_element_type=jnp.float32
    )
    out_grad = lax.dot_general(
        act_low, upstream, (((0,), (0,)), ((), ())), preferred_element_type=jnp.float32
    )
    in_bias = jnp.sum(pre_low, axis=0, dtype=jnp.float32)
    out_bias = jnp.sum(upstream, axis=0, dtype=jnp.float32)
    return (
        branch.reshape(normed_low.shape),
        normed_grad.reshape(normed_low.shape),
        in_grad,
        in_bias,
        out_grad,
        out_bias,
    )


def general(
    fields,
    cotangent,
    kernel,
    norm_gain,
    norm_shift,
    weight_in,
    bias_in,
    weight_out,
    bias_out,
    neighbours,
    land_mask,
):
    position = lax.axis_index("tile")
    devices = lax.axis_size("tile")
    slots = fields.shape[0]
    width = fields.shape[-1]
    ocean = land_mask.astype(jnp.float32)
    cell_weight = ocean[:, :, None]
    arrivals = []
    for offset in range(-REACH, REACH + 1):
        if offset == 0:
            arrivals.append(fields)
        else:
            arrivals.append(from_behind(fields, "tile", -offset))
    stacked = jnp.concatenate(arrivals + [jnp.zeros((1,) + fields.shape[1:], jnp.float32)], axis=0)
    bucket = (2 * REACH + 1) * slots
    source = neighbours // slots - position + REACH
    places = jnp.where(neighbours < 0, bucket, source * slots + neighbours % slots).reshape(-1)
    nearby = jnp.take(stacked, places, axis=0).reshape(slots, 8, TILE_SIDE, TILE_SIDE, width)
    centre = fields.reshape(slots, TILE_SIDE, TILE_SIDE, width)
    conv_tiles, pullback = jax.vjp(depthwise, centre, nearby, kernel)
    conv = conv_tiles.reshape(fields.shape)
    ocean_count, first_sum = lax.psum(
        (jnp.sum(ocean), jnp.sum(conv * cell_weight, axis=(0, 1))), "tile"
    )
    centre_mean = first_sum / ocean_count
    spread = (
        lax.psum(jnp.sum(jnp.square(conv - centre_mean) * cell_weight, axis=(0, 1)), "tile")
        / ocean_count
    )
    inv_spread = lax.rsqrt(spread + EPSILON)
    scaled = (conv - centre_mean) * inv_spread
    normed_low = (scaled * norm_gain + norm_shift).astype(jnp.bfloat16)
    grads_low = (cotangent * cell_weight).astype(jnp.bfloat16)
    branch, normed_grad, in_grad, in_bias, out_grad, out_bias = feed_both(
        normed_low, grads_low, weight_in, bias_in, weight_out, bias_out
    )
    block_out = (fields + branch) * cell_weight
    grad_rows = 8 * devices
    weight_in_grad, weight_out_grad = (
        lax.psum_scatter(in_grad.reshape(grad_rows, -1), "tile", scatter_dimension=0, tiled=True),
        lax.psum_scatter(out_grad.reshape(grad_rows, -1), "tile", scatter_dimension=0, tiled=True),
    )
    shift_part = jnp.sum(normed_grad, axis=(0, 1))
    gain_part = jnp.sum(normed_grad * scaled, axis=(0, 1))
    shift_grad, gain_grad, bias_in_grad, bias_out_grad = lax.psum(
        (shift_part, gain_part, in_bias, out_bias), "tile"
    )
    conv_grad = (
        norm_gain
        * inv_spread
        * (normed_grad - cell_weight * (shift_grad + scaled * gain_grad) / ocean_count)
    )
    centre_grad, nearby_grad, kernel_part = pullback(conv_grad.reshape(centre.shape))
    choose = (places[None, :] == jnp.arange(bucket, dtype=jnp.int32)[:, None]).astype(jnp.float32)
    outgoing = jnp.dot(
        choose, nearby_grad.reshape(slots * 8, -1), precision=lax.Precision.HIGHEST
    ).reshape(2 * REACH + 1, slots, CELLS, width)
    fields_grad = cotangent * cell_weight + centre_grad.reshape(fields.shape) + outgoing[REACH]
    for offset in range(-REACH, REACH + 1):
        if offset != 0:
            fields_grad = fields_grad + from_behind(
                outgoing[offset + REACH].astype(jnp.bfloat16), "tile", offset
            ).astype(jnp.float32)
    kernel_grad = lax.psum(kernel_part, "tile")
    return (
        block_out,
        fields_grad,
        kernel_grad,
        gain_grad,
        shift_grad,
        weight_in_grad,
        bias_in_grad,
        weight_out_grad,
        bias_out_grad,
    )


IN_SPECS = (
    P("tile", None, None),
    P("tile", None, None),
    P(),
    P(),
    P(),
    P(),
    P(),
    P(),
    P(),
    P("tile", None),
    P("tile", None),
)
OUT_SPECS = (
    P("tile", None, None),
    P("tile", None, None),
    P(),
    P(),
    P(),
    P("tile", None),
    P(),
    P("tile", None),
    P(),
)


def solution(mesh):
    N = mesh.shape["tile"]

    def whole(fields, cotangent, kernel, norm_gain, norm_shift, weight_in, *rest):
        C, H = weight_in.shape
        if Sizes.fits(N, C, H) and fields.shape[0] == 2 * N:
            body = functools.partial(local_step, Sizes(N, C, H))
        else:
            body = general
        return jax.shard_map(body, mesh=mesh, in_specs=IN_SPECS, out_specs=OUT_SPECS, check_vma=False)(
            fields, cotangent, kernel, norm_gain, norm_shift, weight_in, *rest
        )

    return whole
```
